256 devices in a mesh: theta: 64 (over z, y_hi, x), rad: 4 (over y_lo, core).
Axes of the slice: x: 4, y: 4 (y_hi: 2, y_lo: 2; y = y_hi * 2 + y_lo), z: 8, core: 2. Of those that a mesh axis runs over, the one named last changes fastest.
Arguments:
- displacement: float32 [3, 768, 128, 320], P(None, 'theta', 'rad'), may hold values from -24 to 24
- stiffness: float32 [768, 128, 320], P('theta', 'rad'), may hold values from 0.1 to 10
- wall: int32 [768, 128, 320], P('theta', 'rad'), may hold values from 0 to 1, as said below
Outputs:
- moved: float32 [3, 768, 128, 320], P(None, 'theta', 'rad')
- residual_norm: float32 [], replicated
The draws below stay inside these ranges and needn't reach their ends.
Inputs may be any that keep to these rules, and one draw needn't show every extreme that they name: wall is 1 on the first and last radial rows and on thin sheared blade surfaces that cross the radial span.
All inputs are finite; a program needn't handle non-finite values.
Results may differ from the reference program's by a relative error of at most 0.00002.
Values sent between devices are 32-bit elements; how exact they have to be, the bound alone decides.
A program may use at most 128 MiB of HBM per device.

```python
import math
import jax
import jax.numpy as jnp
from jax import lax

NA = 320
SWEEPS = 2
NTH = 768
NR = 128


def draw_displacement(key, part):
    key = jax.random.fold_in(key, 5)
    shape = (3, NTH, NR, NA)
    plane_pos = lax.broadcasted_iota(jnp.float32, shape, 1) / float(NTH)
    rough = jnp.clip(jax.random.normal(key, shape, jnp.float32), -4.0, 4.0)
    scale = 0.5 * jnp.exp(plane_pos * 2.0794415)
    return (rough * scale).astype(jnp.float32)


def draw_wall(key, part):
    key = jax.random.fold_in(key, 2)
    blades = max(1, NTH // 48)
    key_start, key_shear, key_band = jax.random.split(key, 3)
    starts = jax.random.randint(key_start, (blades,), 0, NTH, dtype=jnp.int32)
    shears = jax.random.randint(key_shear, (blades,), 2, 5, dtype=jnp.int32)
    bands = jax.random.randint(key_band, (blades,), 0, NA // 4 + 1, dtype=jnp.int32)
    shape = (NTH, NR, NA)
    plane_idx = lax.broadcasted_iota(jnp.int32, shape, 0)
    row_idx = lax.broadcasted_iota(jnp.int32, shape, 1)
    axial_idx = lax.broadcasted_iota(jnp.int32, shape, 2)
    solid = (row_idx == 0) | (row_idx == NR - 1)
    for blade in range(blades):
        target = (starts[blade] + axial_idx * shears[blade] // 64) % NTH
        in_band = (axial_idx >= bands[blade]) & (axial_idx < bands[blade] + NA // 2)
        solid = solid | (plane_idx == target) & in_band
    return solid.astype(jnp.int32)


def level_of(key, extent, cuts, smallest, top_value):
    def one(dim, parts):
        heights = jax.random.uniform(jax.random.fold_in(jax.random.fold_in(key, 6), dim), (parts,), jnp.float32, smallest / len(cuts), top_value / len(cuts))
        return jnp.repeat(jnp.exp(heights), extent[dim] // parts).reshape((-1,) + (1,) * (len(extent) - dim - 1))

    level = one(*cuts[0])
    for cut in cuts[1:]:
        level = level * one(*cut)
    return level


def setup_inputs(seed: int = 0) -> dict:
    splits = jax.random.split(jax.random.key(seed), 4)
    displacement = draw_displacement(jax.random.fold_in(splits[3], 71), 0)
    stiffness = jnp.clip(jnp.exp(math.log(10.0) - 4.6051702 * jax.random.uniform(splits[1], (NTH, NR, NA), jnp.float32) ** level_of(splits[1], (NTH, NR, NA), ((0, 64), (1, 4)), -0.2, 0.2)), 0.1, 10.0)
    wall = draw_wall(jax.random.fold_in(splits[3], 71), 0)
    return {"displacement": displacement, "stiffness": stiffness, "wall": wall}


RELAX_FACTOR = 1.5

def around_ref(values, mode):
    padding = [(0, 0)] * (values.ndim - 2) + [(1, 1), (1, 1)]
    padded = jnp.pad(values, padding, mode=mode)
    neighbours = [jnp.roll(values, -1, axis=-3), jnp.roll(values, 1, axis=-3), padded[..., 2:, 1:-1], padded[..., :-2, 1:-1], padded[..., 1:-1, 2:], padded[..., 1:-1, :-2]]
    return neighbours

def averaged(field, weights, total_weight):
    neighbours = around_ref(field, 'constant')
    weighted = weights[0] * neighbours[0]
    for index in range(1, 6):
        weighted = weighted + weights[index] * neighbours[index]
    return weighted / total_weight

def reference(displacement, stiffness, wall):
    shape = (NTH, NR, NA)
    parity = (lax.broadcasted_iota(jnp.int32, shape, 0) + lax.broadcasted_iota(jnp.int32, shape, 1) + lax.broadcasted_iota(jnp.int32, shape, 2)) % 2
    coeff_near = around_ref(stiffness, 'edge')
    weights = [0.5 * (stiffness + other) for other in coeff_near]
    total_weight = weights[0]
    for index in range(1, 6):
        total_weight = total_weight + weights[index]
    field = displacement
    for sweep in range(SWEEPS):
        for shade in range(2):
            chosen = (parity == shade) & (wall == 0)
            average = averaged(field, weights, total_weight)
            updated = field + RELAX_FACTOR * (average - field)
            field = jnp.where(chosen, updated, field)
    residual = averaged(field, weights, total_weight) - field
    residual = jnp.where(wall == 0, residual, 0.0)
    count = 3.0 * NTH * NR * NA
    residual_norm = jnp.sqrt(jnp.sum(residual * residual) / count)
    return (field, residual_norm)
```

```python
import functools

import jax
import jax.numpy as jnp
from jax import lax
from jax.experimental import pallas as pl
from jax.experimental.pallas import tpu as pltpu
from jax.sharding import PartitionSpec as P

MESH = pl.DeviceIdType.MESH
F32 = jnp.float32
LANES = 128
OFF = 8
NAMES = ("self", "in", "out", "rp", "rm", "ap", "am")
SELF, IN, OUT, RP, RM, AP, AM = range(7)


def iota(dim):
    return lax.broadcasted_iota(jnp.int32, (8, LANES), dim)


def kernel(
    cfg, d_hbm, s_hbm, w_hbm, out_hbm, norm_ref,
    raw_d, raw_s, raw_w, field, stiff, weight, stage, land, edge_s, part, gather,
    load_sem, out_sem, th_send, th_recv, es_send, es_recv, rd_send, rd_recv, rs_send, rs_recv, ar_send, ar_recv,
):
    n_theta, n_rad, pairs, rows, cols, tiles, levels, count = cfg
    t, r = lax.axis_index("theta"), lax.axis_index("rad")
    tile_rows = rows // 8
    last_lanes = cols - (tiles - 1) * LANES
    nxt, prv = (lax.rem(t + 1, n_theta), r), (lax.rem(t + n_theta - 1, n_theta), r)
    above, below = (t, jnp.minimum(r + 1, n_rad - 1)), (t, jnp.maximum(r - 1, 0))
    has_above, has_below = r < n_rad - 1, r > 0

    loads = [
        pltpu.make_async_copy(s_hbm, raw_s, load_sem.at[0]),
        pltpu.make_async_copy(w_hbm, raw_w, load_sem.at[1]),
        pltpu.make_async_copy(d_hbm, raw_d, load_sem.at[2]),
    ]
    for c in loads:
        c.start()

    groups = [level(t, r) for level in levels]
    barrier = pltpu.get_barrier_semaphore()
    greet = [nxt, prv] + [p for g in groups for p in g]
    for p in greet:
        pl.semaphore_signal(barrier, inc=1, device_id=p, device_id_type=MESH)

    even = (iota(0) + iota(1)) % 2 == 0
    first_lane, last_lane = iota(1) == 0, iota(1) == LANES - 1
    inside = iota(1) < last_lanes
    at_first_col, at_last_col = iota(1) == 0, iota(1) == last_lanes - 1

    def raw_tile(ref, lead, i, q):
        if q < tiles - 1:
            return ref[(*lead, pl.ds(8 * i, 8), pl.ds(q * LANES, LANES))]
        x = ref[(*lead, pl.ds(8 * i, 8), pl.ds(q * LANES, last_lanes))]
        if last_lanes == LANES:
            return x
        return jnp.concatenate([x, jnp.zeros((8, LANES - last_lanes), x.dtype)], axis=1)

    def at(i, shift=0):
        return pl.ds(OFF + 8 * i + shift, 8)

    zero_row = jnp.zeros((1, LANES), F32)
    loads[0].wait()

    def pack_s(k, _):
        for i in range(tile_rows):
            for q in range(tiles):
                a, b = raw_tile(raw_s, (2 * k,), i, q), raw_tile(raw_s, (2 * k + 1,), i, q)
                stiff[0, k + 1, q, at(i), :] = jnp.where(even, a, b)
                stiff[1, k + 1, q, at(i), :] = jnp.where(even, b, a)
        return 0

    lax.fori_loop(0, pairs, pack_s, 0)
    loads[2].wait()

    def pack_d(j, _):
        c, k = j // pairs, j % pairs
        for i in range(tile_rows):
            for q in range(tiles):
                a, b = raw_tile(raw_d, (c, 2 * k), i, q), raw_tile(raw_d, (c, 2 * k + 1), i, q)
                field[0, c, k + 1, q, at(i), :] = jnp.where(even, a, b)
                field[1, c, k + 1, q, at(i), :] = jnp.where(even, b, a)
        return 0

    lax.fori_loop(0, 3 * pairs, pack_d, 0)
    loads[1].wait()

    @pl.when(jnp.logical_not(has_below))
    def _():
        for colour in range(2):
            for k in range(pairs):
                for q in range(tiles):
                    stiff[colour, k + 1, q, pl.ds(OFF - 1, 1), :] = zero_row
                    for c in range(3):
                        field[colour, c, k + 1, q, pl.ds(OFF - 1, 1), :] = zero_row

    @pl.when(jnp.logical_not(has_above))
    def _():
        for colour in range(2):
            for k in range(pairs):
                for q in range(tiles):
                    stiff[colour, k + 1, q, pl.ds(OFF + rows, 1), :] = zero_row
                    for c in range(3):
                        field[colour, c, k + 1, q, pl.ds(OFF + rows, 1), :] = zero_row

    def theta_copies(n):
        return [
            pltpu.make_async_remote_copy(
                stage.at[n, side], land.at[n, 1 - side], th_send.at[n, side], th_recv.at[n, 1 - side],
                device_id=p, device_id_type=MESH,
            )
            for side, p in ((0, prv), (1, nxt))
        ]

    def send_theta(n, colour):
        for side in range(2):
            k = 1 if side == 0 else pairs
            keep = even if side == colour else jnp.logical_not(even)
            for c in range(3):
                for q in range(tiles):
                    for h in range(tile_rows // 2):
                        a = field[colour, c, k, q, at(2 * h), :]
                        b = field[colour, c, k, q, at(2 * h + 1), :]
                        stage[n, side, c, q, pl.ds(8 * h, 8), :] = jnp.where(keep, a, pltpu.roll(b, 1, 0))
        for copy in theta_copies(n):
            copy.start()

    def take_theta(n, colour):
        for copy in theta_copies(n):
            copy.wait_recv()
        for side in range(2):
            k = 0 if side == 0 else pairs + 1
            for c in range(3):
                for q in range(tiles):
                    for h in range(tile_rows // 2):
                        x = land[n, side, c, q, pl.ds(8 * h, 8), :]
                        field[colour, c, k, q, at(2 * h), :] = x
                        field[colour, c, k, q, at(2 * h + 1), :] = pltpu.roll(x, 7, 0)

    own = pl.ds(1, pairs)

    def rad_copy(ref, lead, up, send, recv):
        src, dst = (OFF + rows - 1, OFF - 1) if up else (OFF, OFF + rows)
        return pltpu.make_async_remote_copy(
            ref.at[(*lead, own, slice(None), pl.ds(src, 1))], ref.at[(*lead, own, slice(None), pl.ds(dst, 1))],
            send, recv, device_id=above if up else below, device_id_type=MESH,
        )

    def field_copy(n, colour, up):
        return rad_copy(field, (colour, slice(None)), up, rd_send.at[n, up], rd_recv.at[n, up])

    def stiff_copy(colour, up):
        return rad_copy(stiff, (colour,), up, rs_send.at[colour, up], rs_recv.at[colour, up])

    def send_rad(copy):
        @pl.when(has_above)
        def _():
            copy(1).start()

        @pl.when(has_below)
        def _():
            copy(0).start()

    def take_rad(copy):
        @pl.when(has_below)
        def _():
            copy(1).wait_recv()

        @pl.when(has_above)
        def _():
            copy(0).wait_recv()

    def drain_rad(copy):
        @pl.when(has_above)
        def _():
            copy(1).wait_send()

        @pl.when(has_below)
        def _():
            copy(0).wait_send()

    edge_copies = [
        pltpu.make_async_remote_copy(
            raw_s.at[0 if side == 0 else 2 * pairs - 1], edge_s.at[1 - side], es_send.at[side], es_recv.at[1 - side],
            device_id=p, device_id_type=MESH,
        )
        for side, p in ((0, prv), (1, nxt))
    ]

    pl.semaphore_wait(barrier, len(greet))
    for copy in edge_copies:
        copy.start()
    for colour in range(2):
        send_rad(functools.partial(stiff_copy, colour))
    send_theta(0, 1)
    send_rad(functools.partial(field_copy, 0, 1))

    def beside(v, w, side):
        out = []
        for q in range(tiles):
            if side:
                x = pltpu.roll(v[q], LANES - 1, 1)
                if q < tiles - 1:
                    x = jnp.where(last_lane, pltpu.roll(v[q + 1], LANES - 1, 1), x)
            else:
                x = pltpu.roll(v[q], 1, 1)
                if q > 0:
                    x = jnp.where(first_lane, pltpu.roll(v[q - 1], 1, 1), x)
            out.append(x)
        return out

    def outer(colour, before, after):
        return jnp.where(even, before, after) if colour == 0 else jnp.where(even, after, before)

    def make_weights(colour, k):
        other = 1 - colour
        for i in range(tile_rows):
            mid = [stiff[other, k + 1, q, at(i), :] for q in range(tiles)]
            forth, back = beside(mid, None, 1), beside(mid, None, 0)
            for q in range(tiles):
                s = stiff[colour, k + 1, q, at(i), :]
                faces = [None] * 7
                faces[IN] = s + mid[q]
                faces[OUT] = s + outer(colour, stiff[other, k, q, at(i), :], stiff[other, k + 2, q, at(i), :])
                faces[RP] = s + stiff[other, k + 1, q, at(i, 1), :]
                faces[RM] = s + stiff[other, k + 1, q, at(i, -1), :]
                ap, am = forth[q], back[q]
                if q == tiles - 1:
                    ap = jnp.where(at_last_col, s, ap)
                if q == 0:
                    am = jnp.where(at_first_col, s, am)
                faces[AP], faces[AM] = s + ap, s + am
                total = faces[IN] + faces[OUT] + (faces[RP] + faces[RM]) + (faces[AP] + faces[AM])
                wa, wb = raw_tile(raw_w, (2 * k,), i, q), raw_tile(raw_w, (2 * k + 1,), i, q)
                fixed = (jnp.where(even, wa, wb) if colour == 0 else jnp.where(even, wb, wa)) != 0
                if q == tiles - 1 and last_lanes < LANES:
                    fixed = jnp.logical_or(fixed, jnp.logical_not(inside))
                scale = jnp.where(fixed, 0.0, 1.5 / total)
                put = pl.ds(8 * i, 8)
                weight[colour, SELF, k, q, put, :] = jnp.where(fixed, 1.0, -0.5)
                for f in (IN, OUT, RP, RM, AP, AM):
                    w = faces[f] * scale
                    if f == AP and q == tiles - 1:
                        w = jnp.where(at_last_col, 0.0, w)
                    if f == AM and q == 0:
                        w = jnp.where(at_first_col, 0.0, w)
                    weight[colour, f, k, q, put, :] = w

    def half(colour, k, mode, acc):
        other = 1 - colour
        for i in range(tile_rows):
            put = pl.ds(8 * i, 8)
            w = [[weight[colour, f, k, q, put, :] for q in range(tiles)] for f in range(7)]
            for c in range(3):
                mid = [field[other, c, k + 1, q, at(i), :] for q in range(tiles)]
                forth, back = beside(mid, None, 1), beside(mid, None, 0)
                for q in range(tiles):
                    far = outer(colour, field[other, c, k, q, at(i), :], field[other, c, k + 2, q, at(i), :])
                    old = field[colour, c, k + 1, q, at(i), :]
                    new = w[SELF][q] * old + w[IN][q] * mid[q] + w[OUT][q] * far
                    new = new + w[RP][q] * field[other, c, k + 1, q, at(i, 1), :]
                    new = new + w[RM][q] * field[other, c, k + 1, q, at(i, -1), :]
                    new = new + w[AP][q] * forth[q] + w[AM][q] * back[q]
                    if mode < 2:
                        field[colour, c, k + 1, q, at(i), :] = new
                    if mode > 0:
                        change = new - old
                        acc = acc + change * change
        return acc

    def over(lo, hi, fn, acc):
        return lax.fori_loop(lo, hi, fn, acc)

    zero = jnp.zeros((8, LANES), F32)
    sums = [zero, zero]
    for n in range(5):
        colour, seen = n % 2, 1 - n % 2
        mode = (0, 0, 0, 1, 2)[n]
        if n > 0:
            drain_rad(functools.partial(field_copy, n - 1, colour))
        if n == 0:
            for col in range(2):
                take_rad(functools.partial(stiff_copy, col))

            def inner_weights(k, _):
                make_weights(0, k)
                make_weights(1, k)
                return 0

            lax.fori_loop(1, pairs - 1, inner_weights, 0)
        take_rad(functools.partial(field_copy, n, seen))
        acc = over(1, pairs - 1, lambda k, a: half(colour, k, mode, a), zero)
        if n == 0:
            for copy in edge_copies:
                copy.wait_recv()
            for side in range(2):
                for i in range(tile_rows):
                    for q in range(tiles):
                        x = raw_tile(edge_s, (side,), i, q)
                        k = 0 if side == 0 else pairs + 1
                        stiff[0, k, q, at(i), :] = x
                        stiff[1, k, q, at(i), :] = x

            def outer_weights(j, _):
                make_weights(0, j * (pairs - 1))
                make_weights(1, j * (pairs - 1))
                return 0

            lax.fori_loop(0, 2, outer_weights, 0)
        take_theta(n, seen)
        acc = over(0, 2, lambda j, a: half(colour, j * (pairs - 1), mode, a), acc)
        if n < 4:
            send_theta(n + 1, colour)
            send_rad(functools.partial(field_copy, n + 1, colour))
        if mode == 1:
            sums[1] = acc
        if mode == 2:
            sums[0] = acc

    part[0] = sums[1] * (1.0 / 9.0) + sums[0] * (1.0 / 2.25)
    for level, peers in enumerate(groups):
        for j, p in enumerate(peers):
            pltpu.make_async_remote_copy(
                part.at[level], gather.at[level, j], ar_send.at[level], ar_recv.at[level], device_id=p, device_id_type=MESH
            ).start()
        if level == 0:
            def unpack(j, _):
                c, k = j // pairs, j % pairs
                for i in range(tile_rows):
                    for q in range(tiles):
                        a, b = field[0, c, k + 1, q, at(i), :], field[1, c, k + 1, q, at(i), :]
                        x, y = jnp.where(even, a, b), jnp.where(even, b, a)
                        n = LANES if q < tiles - 1 else last_lanes
                        raw_d[c, 2 * k, pl.ds(8 * i, 8), pl.ds(q * LANES, n)] = x[:, :n]
                        raw_d[c, 2 * k + 1, pl.ds(8 * i, 8), pl.ds(q * LANES, n)] = y[:, :n]
                return 0

            lax.fori_loop(0, 3 * pairs, unpack, 0)
            pltpu.make_async_copy(raw_d, out_hbm, out_sem.at[0]).start()
        everything = gather.at[level, pl.ds(0, len(peers))]
        pltpu.make_async_copy(everything, everything, ar_recv.at[level]).wait()
        part[level + 1] = part[level] + jnp.sum(gather[level, : len(peers)], axis=0)
    norm_ref[...] = jnp.sqrt(jnp.sum(part[len(groups)], keepdims=True) / count)

    for level, peers in enumerate(groups):
        everything = gather.at[level, pl.ds(0, len(peers))]
        pltpu.make_async_copy(everything, everything, ar_send.at[level]).wait()
    for copy in edge_copies:
        copy.wait_send()
    for colour in range(2):
        drain_rad(functools.partial(stiff_copy, colour))
    for n in range(5):
        for copy in theta_copies(n):
            copy.wait_send()
    drain_rad(functools.partial(field_copy, 4, 1))
    pltpu.make_async_copy(raw_d, out_hbm, out_sem.at[0]).wait()


def make_levels(n_theta, n_rad):
    plane = 8 if n_theta % 8 == 0 else n_theta
    stacks = n_theta // plane

    def within(t, r):
        z, x = t // plane, lax.rem(t, plane)
        return [
            (z * plane + lax.rem(x + i, plane), lax.rem(r + j, n_rad))
            for j in range(n_rad) for i in range(plane) if i or j
        ]

    def across(t, r):
        return [(lax.rem(t + i * plane, n_theta), r) for i in range(1, stacks)]

    return (within, across), (n_rad * plane - 1, stacks - 1)


def solution(mesh):
    n_theta, n_rad = mesh.shape["theta"], mesh.shape["rad"]
    levels, sizes = make_levels(n_theta, n_rad)

    def shards(displacement, stiffness, wall):
        planes, rows, cols = stiffness.shape
        pairs, tiles = planes // 2, -(-cols // LANES)
        count = 3.0 * planes * rows * cols * n_theta * n_rad
        cfg = (n_theta, n_rad, pairs, rows, cols, tiles, levels, count)
        dma = pltpu.SemaphoreType.DMA
        moved, norm = pl.pallas_call(
            functools.partial(kernel, cfg),
            out_shape=(jax.ShapeDtypeStruct(displacement.shape, F32), jax.ShapeDtypeStruct((1, 1), F32)),
            in_specs=[pl.BlockSpec(memory_space=pl.ANY)] * 3,
            out_specs=(pl.BlockSpec(memory_space=pl.ANY), pl.BlockSpec(memory_space=pltpu.VMEM)),
            scratch_shapes=[
                pltpu.VMEM((3, planes, rows, cols), F32),
                pltpu.VMEM((planes, rows, cols), F32),
                pltpu.VMEM((planes, rows, cols), jnp.int32),
                pltpu.VMEM((2, 3, pairs + 2, tiles, rows + 16, LANES), F32),
                pltpu.VMEM((2, pairs + 2, tiles, rows + 16, LANES), F32),
                pltpu.VMEM((2, 7, pairs, tiles, rows, LANES), F32),
                pltpu.VMEM((5, 2, 3, tiles, rows // 2, LANES), F32),
                pltpu.VMEM((5, 2, 3, tiles, rows // 2, LANES), F32),
                pltpu.VMEM((2, rows, cols), F32),
                pltpu.VMEM((3, 8, LANES), F32),
                pltpu.VMEM((2, max(sizes), 8, LANES), F32),
                dma((3,)), dma((1,)), dma((5, 2)), dma((5, 2)), dma((2,)), dma((2,)),
                dma((5, 2)), dma((5, 2)), dma((2, 2)), dma((2, 2)), dma((2,)), dma((2,)),
            ],
            compiler_params=pltpu.CompilerParams(collective_id=0, has_side_effects=True, vmem_limit_bytes=48 * 2**20),
            cost_estimate=pl.CostEstimate(flops=10**8, bytes_accessed=4 * 10**6, transcendentals=0),
        )(displacement, stiffness, wall)
        return moved, norm.reshape(())

    placed = (P(None, "theta", "rad", None), P("theta", "rad", None), P("theta", "rad", None))
    return jax.shard_map(
        shards, mesh=mesh, in_specs=placed, out_specs=(P(None, "theta", "rad", None), P()), check_vma=False,
    )
```

```python
import functools

import jax
import jax.numpy as jnp
from jax import lax
from jax.experimental import pallas as pl
from jax.experimental.pallas import tpu as pltpu
from jax.sharding import PartitionSpec as P

MESH = pl.DeviceIdType.MESH
F32 = jnp.float32
LANES = 128
OFF = 8
SELF, IN, OUT, RP, RM, AP, AM = range(7)


def iota(dim):
    return lax.broadcasted_iota(jnp.int32, (8, LANES), dim)


def kernel(
    cfg, d_hbm, s_hbm, w_hbm, out_hbm, norm_ref,
    raw_d, raw_s, raw_w, field, last, stiff, weight, scale_b, first_out, first_in, stage, land, land_g,
    rad_in, rad_g, corner, edge_s, edge_c, w_theta, w_rad, w_face, w_corner, part, gather,
    load_sem, out_sem, f_send, f_recv, t_send, t_recv, g_send, g_recv, es_send, es_recv, ec_send, ec_recv,
    rs_send, rs_recv, r0_send, r0_recv, rd_send, rd_recv, rg_send, rg_recv, c_send, c_recv, ar_send, ar_recv,
):
    n_theta, n_rad, pairs, rows, cols, tiles, levels, count = cfg
    t, r = lax.axis_index("theta"), lax.axis_index("rad")
    tile_rows = rows // 8
    last_lanes = cols - (tiles - 1) * LANES
    t_next, t_prev = lax.rem(t + 1, n_theta), lax.rem(t + n_theta - 1, n_theta)
    r_up, r_down = lax.rem(r + 1, n_rad), lax.rem(r + n_rad - 1, n_rad)
    beside_t = (t_prev, t_next)
    beside_r = (r_down, r_up)
    has = (r > 0, r < n_rad - 1)
    rim = (1, pairs)
    ghost = (0, pairs + 1)
    edge_row = (OFF, OFF + rows - 1)
    beyond = (OFF - 1, OFF + rows)
    own = pl.ds(1, pairs)

    loads = [
        pltpu.make_async_copy(s_hbm, raw_s, load_sem.at[0]),
        pltpu.make_async_copy(d_hbm, raw_d, load_sem.at[1]),
        pltpu.make_async_copy(w_hbm, raw_w, load_sem.at[2]),
    ]
    for c in loads:
        c.start()

    groups = [level(t, r) for level in levels]
    barrier = pltpu.get_barrier_semaphore()
    diagonal = [(tt, rr) for tt in beside_t for rr in beside_r]
    greet = [(tt, r) for tt in beside_t] + diagonal + [p for g in groups for p in g]
    for p in greet:
        pl.semaphore_signal(barrier, inc=1, device_id=p, device_id_type=MESH)

    even = (iota(0) + iota(1)) % 2 == 0
    odd = jnp.logical_not(even)
    lane = lax.broadcasted_iota(jnp.int32, (1, LANES), 1)
    first_lane, last_lane = iota(1) == 0, iota(1) == LANES - 1
    inside = iota(1) < last_lanes
    at_first_col, at_last_col = iota(1) == 0, iota(1) == last_lanes - 1

    def facing(colour, side):
        return even if colour == side else odd

    def raw_tile(ref, lead, i, q):
        if q < tiles - 1:
            return ref[(*lead, pl.ds(8 * i, 8), pl.ds(q * LANES, LANES))]
        x = ref[(*lead, pl.ds(8 * i, 8), pl.ds(q * LANES, last_lanes))]
        if last_lanes == LANES:
            return x
        return jnp.concatenate([x, jnp.zeros((8, LANES - last_lanes), x.dtype)], axis=1)

    def raw_row(ref, lead, q):
        if q < tiles - 1:
            return ref[(*lead, pl.ds(0, 1), pl.ds(q * LANES, LANES))]
        x = ref[(*lead, pl.ds(0, 1), pl.ds(q * LANES, last_lanes))]
        if last_lanes == LANES:
            return x
        return jnp.concatenate([x, jnp.zeros((1, LANES - last_lanes), x.dtype)], axis=1)

    def at(i, shift=0):
        return pl.ds(OFF + 8 * i + shift, 8)

    def one(row):
        return pl.ds(row, 1)

    zero_row = jnp.zeros((1, LANES), F32)
    zero = jnp.zeros((8, LANES), F32)
    loads[0].wait()

    def pack_s(k, _):
        for i in range(tile_rows):
            for q in range(tiles):
                a, b = raw_tile(raw_s, (2 * k,), i, q), raw_tile(raw_s, (2 * k + 1,), i, q)
                stiff[0, k + 1, q, at(i), :] = jnp.where(even, a, b)
                stiff[1, k + 1, q, at(i), :] = jnp.where(even, b, a)
        return 0

    lax.fori_loop(0, pairs, pack_s, 0)
    loads[1].wait()

    def pack_d(j, _):
        c, k = j // pairs, j % pairs
        for i in range(tile_rows):
            for q in range(tiles):
                a, b = raw_tile(raw_d, (c, 2 * k), i, q), raw_tile(raw_d, (c, 2 * k + 1), i, q)
                field[0, c, k + 1, q, at(i), :] = jnp.where(even, a, b)
                field[1, c, k + 1, q, at(i), :] = jnp.where(even, b, a)
        for q in range(tiles):
            for row in beyond:
                field[0, c, k + 1, q, one(row), :] = zero_row
                last[c, k + 1, q, one(row), :] = zero_row
        return 0

    lax.fori_loop(0, 3 * pairs, pack_d, 0)
    for end in range(2):
        @pl.when(jnp.logical_not(has[end]))
        def _():
            def clear(k, _):
                for q in range(tiles):
                    stiff[0, k + 1, q, one(beyond[end]), :] = zero_row
                    stiff[1, k + 1, q, one(beyond[end]), :] = zero_row
                    for c in range(3):
                        field[1, c, k + 1, q, one(beyond[end]), :] = zero_row
                return 0

            lax.fori_loop(0, pairs, clear, 0)

    for c in range(3):
        for g in ghost:
            for q in range(tiles):
                for i in range(tile_rows):
                    field[0, c, g, q, at(i), :] = zero
    loads[2].wait()

    def to(tt, rr):
        return {"device_id": (tt, rr), "device_id_type": MESH}

    def remote(src, dst, send, recv, where):
        return pltpu.make_async_remote_copy(src, dst, send, recv, **where)

    edge_copies = [
        remote(raw_s.at[0 if side == 0 else 2 * pairs - 1], edge_s.at[1 - side], es_send.at[side], es_recv.at[1 - side], to(beside_t[side], r))
        for side in range(2)
    ]
    first_copies = [
        remote(first_out.at[side], first_in.at[1 - side], f_send.at[side], f_recv.at[1 - side], to(beside_t[side], r))
        for side in range(2)
    ]

    def theta_copies(n):
        return [
            remote(stage.at[n, side], land.at[n, 1 - side], t_send.at[n, side], t_recv.at[n, 1 - side], to(beside_t[side], r))
            for side in range(2)
        ]

    g_copies = [
        remote(scale_b.at[rim[side] - 1], land_g.at[1 - side], g_send.at[side], g_recv.at[1 - side], to(beside_t[side], r))
        for side in range(2)
    ]

    def stiff_rows(end):
        return [
            remote(
                stiff.at[colour, own, slice(None), one(edge_row[end])], stiff.at[colour, own, slice(None), one(beyond[1 - end])],
                rs_send.at[colour, end], rs_recv.at[colour, 1 - end], to(t, beside_r[end]),
            )
            for colour in range(2)
        ]

    def edge_corners(end):
        return [
            remote(
                raw_s.at[0 if side == 0 else 2 * pairs - 1, pl.ds(0 if end == 0 else rows - 1, 1)], edge_c.at[1 - side, 1 - end],
                ec_send.at[side, end], ec_recv.at[1 - side, 1 - end], to(beside_t[side], beside_r[end]),
            )
            for side in range(2)
        ]

    def first_rows(end):
        return [
            remote(
                field.at[1, slice(None), own, slice(None), one(edge_row[end])], field.at[1, slice(None), own, slice(None), one(beyond[1 - end])],
                r0_send.at[end], r0_recv.at[1 - end], to(t, beside_r[end]),
            )
        ]

    def black(n):
        return field.at[1] if n == 0 else last

    def both_rows(n, end):
        return [
            remote(
                ref.at[slice(None), own, slice(None), one(edge_row[end])], rad_in.at[n, colour, 1 - end],
                rd_send.at[n, colour, end], rd_recv.at[n, colour, 1 - end], to(t, beside_r[end]),
            )
            for colour, ref in ((0, field.at[0]), (1, black(n)))
        ]

    def scale_rows(end):
        return [
            remote(
                scale_b.at[slice(None), slice(None), one(edge_row[end] - OFF)], rad_g.at[1 - end],
                rg_send.at[end], rg_recv.at[1 - end], to(t, beside_r[end]),
            )
        ]

    def red_corners(n, end):
        return [
            remote(
                field.at[0, slice(None), rim[side], slice(None), one(edge_row[end])], corner.at[n, 1 - side, 1 - end],
                c_send.at[n, side, end], c_recv.at[n, 1 - side, 1 - end], to(beside_t[side], beside_r[end]),
            )
            for side in range(2)
        ]

    def by_end(copies, what):
        for end in range(2):
            @pl.when(has[end])
            def _():
                for copy in copies(end if what != "take" else 1 - end):
                    if what == "start":
                        copy.start()
                    elif what == "take":
                        copy.wait_recv()
                    else:
                        copy.wait_send()

    def send_first():
        for side in range(2):
            keep = facing(1, side)
            for c in range(3):
                for q in range(tiles):
                    for h in range(tile_rows // 2):
                        a = field[1, c, rim[side], q, at(2 * h), :]
                        b = field[1, c, rim[side], q, at(2 * h + 1), :]
                        first_out[side, c, q, pl.ds(8 * h, 8), :] = jnp.where(keep, a, pltpu.roll(b, 1, 0))
        for copy in first_copies:
            copy.start()

    def take_first():
        for copy in first_copies:
            copy.wait_recv()
        for side in range(2):
            for c in range(3):
                for q in range(tiles):
                    for h in range(tile_rows // 2):
                        x = first_in[side, c, q, pl.ds(8 * h, 8), :]
                        field[1, c, ghost[side], q, at(2 * h), :] = x
                        field[1, c, ghost[side], q, at(2 * h + 1), :] = pltpu.roll(x, 7, 0)

    def send_theta(n):
        for side in range(2):
            red_here = facing(0, side)
            for c in range(3):
                for q in range(tiles):
                    for i in range(tile_rows):
                        x = field[0, c, rim[side], q, at(i), :]
                        y = black(n)[c, rim[side], q, at(i), :]
                        stage[n, side, c, q, pl.ds(8 * i, 8), :] = jnp.where(red_here, x, y)
        for copy in theta_copies(n):
            copy.start()
        by_end(functools.partial(red_corners, n), "start")

    pl.semaphore_wait(barrier, len(greet))
    for copy in edge_copies:
        copy.start()
    send_first()
    by_end(stiff_rows, "start")
    by_end(first_rows, "start")
    by_end(edge_corners, "start")

    def beside(v, side):
        out = []
        for q in range(tiles):
            if side:
                x = pltpu.roll(v[q], LANES - 1, 1)
                if q < tiles - 1:
                    x = jnp.where(last_lane, pltpu.roll(v[q + 1], LANES - 1, 1), x)
            else:
                x = pltpu.roll(v[q], 1, 1)
                if q > 0:
                    x = jnp.where(first_lane, pltpu.roll(v[q - 1], 1, 1), x)
            out.append(x)
        return out

    def outer(colour, before, after):
        return jnp.where(even, before, after) if colour == 0 else jnp.where(even, after, before)

    def make_weights(colour, k):
        other = 1 - colour
        for i in range(tile_rows):
            mid = [stiff[other, k + 1, q, at(i), :] for q in range(tiles)]
            forth, back = beside(mid, 1), beside(mid, 0)
            for q in range(tiles):
                s = stiff[colour, k + 1, q, at(i), :]
                faces = [None] * 7
                faces[IN] = s + mid[q]
                faces[OUT] = s + outer(colour, stiff[other, k, q, at(i), :], stiff[other, k + 2, q, at(i), :])
                faces[RP] = s + stiff[other, k + 1, q, at(i, 1), :]
                faces[RM] = s + stiff[other, k + 1, q, at(i, -1), :]
                ap, am = forth[q], back[q]
                if q == tiles - 1:
                    ap = jnp.where(at_last_col, s, ap)
                if q == 0:
                    am = jnp.where(at_first_col, s, am)
                faces[AP], faces[AM] = s + ap, s + am
                total = faces[IN] + faces[OUT] + (faces[RP] + faces[RM]) + (faces[AP] + faces[AM])
                wa, wb = raw_tile(raw_w, (2 * k,), i, q), raw_tile(raw_w, (2 * k + 1,), i, q)
                fixed = (jnp.where(even, wa, wb) if colour == 0 else jnp.where(even, wb, wa)) != 0
                if q == tiles - 1 and last_lanes < LANES:
                    fixed = jnp.logical_or(fixed, jnp.logical_not(inside))
                scale = jnp.where(fixed, 0.0, 1.5 / total)
                put = pl.ds(8 * i, 8)
                if colour == 1:
                    scale_b[k, q, put, :] = scale
                weight[colour, SELF, k, q, put, :] = jnp.where(fixed, 1.0, -0.5)
                for f in (IN, OUT, RP, RM, AP, AM):
                    w = faces[f] * scale
                    if f == AP and q == tiles - 1:
                        w = jnp.where(at_last_col, 0.0, w)
                    if f == AM and q == 0:
                        w = jnp.where(at_first_col, 0.0, w)
                    weight[colour, f, k, q, put, :] = w

    def half(colour, k, opp, cur, dst, acc=None):
        for i in range(tile_rows):
            put = pl.ds(8 * i, 8)
            w = [[weight[colour, f, k, q, put, :] for q in range(tiles)] for f in range(7)]
            for c in range(3):
                mid = [opp[c, k + 1, q, at(i), :] for q in range(tiles)]
                forth, back = beside(mid, 1), beside(mid, 0)
                for q in range(tiles):
                    far = outer(colour, opp[c, k, q, at(i), :], opp[c, k + 2, q, at(i), :])
                    old = cur[c, k + 1, q, at(i), :]
                    new = w[SELF][q] * old + w[IN][q] * mid[q] + w[OUT][q] * far
                    new = new + w[RP][q] * opp[c, k + 1, q, at(i, 1), :]
                    new = new + w[RM][q] * opp[c, k + 1, q, at(i, -1), :]
                    new = new + w[AP][q] * forth[q] + w[AM][q] * back[q]
                    if dst is not None:
                        dst[c, k + 1, q, at(i), :] = new
                    if acc is not None:
                        change = new - old
                        acc = acc + change * change
        return acc

    def inner(fn):
        lax.fori_loop(1, pairs - 1, lambda k, _: (fn(k), 0)[1], 0)

    def rims(fn):
        lax.fori_loop(0, 2, lambda j, _: (fn(j * (pairs - 1)), 0)[1], 0)

    def face_weights():
        for side in range(2):
            k = rim[side]
            for q in range(tiles):
                for i in range(tile_rows):
                    put = pl.ds(8 * i, 8)
                    w_theta[side, q, put, :] = (stiff[1, ghost[side], q, at(i), :] + stiff[0, k, q, at(i), :]) * land_g[side, q, put, :]
        for end in range(2):
            @pl.when(has[end])
            def _():
                for q in range(tiles):
                    for side in range(2):
                        s = stiff[1, ghost[side], q, one(edge_row[end]), :]
                        g = land_g[side, q, one(edge_row[end] - OFF), :]
                        x = raw_row(edge_c, (side, end), q)
                        w_corner[side, end, q] = (s + x) * g
                        k = rim[side]
                        parity = (beyond[end] + lane) % 2 == 0
                        here = parity if side == 1 else jnp.logical_not(parity)
                        w_face[side, end, q] = jnp.where(here, (stiff[1, k, q, one(beyond[end]), :] + x) * rad_g[end, k - 1, q], 0.0)

    def rad_weights():
        for end in range(2):
            @pl.when(has[end])
            def _():
                def body(k, _):
                    for q in range(tiles):
                        w_rad[end, k, q] = (stiff[1, k + 1, q, one(beyond[end]), :] + stiff[0, k + 1, q, one(edge_row[end]), :]) * rad_g[end, k, q]
                    return 0

                lax.fori_loop(0, pairs, body, 0)

    def cross_rad(n):
        dst = black(n)
        for end in range(2):
            @pl.when(has[end])
            def _():
                f = RP if end else RM

                def body(k, _):
                    for q in range(tiles):
                        w = weight[1, f, k, q, one(edge_row[end] - OFF), :]
                        wg = w_rad[end, k, q]
                        for c in range(3):
                            here = (c, k + 1, q, one(edge_row[end]), slice(None))
                            dst[here] = dst[here] + w * rad_in[n, 0, end, c, k, q]
                            dst[c, k + 1, q, one(beyond[end]), :] = rad_in[n, 1, end, c, k, q] + wg * field[(0, *here)]
                    return 0

                lax.fori_loop(0, pairs, body, 0)

    def cross_theta(n):
        dst = black(n)
        for side in range(2):
            k, here = rim[side], facing(1, side)
            for q in range(tiles):
                for i in range(tile_rows):
                    put = pl.ds(8 * i, 8)
                    w = jnp.where(here, weight[1, OUT, k - 1, q, put, :], 0.0)
                    wg = w_theta[side, q, put, :]
                    for c in range(3):
                        x = land[n, side, c, q, put, :]
                        dst[c, k, q, at(i), :] = dst[c, k, q, at(i), :] + w * x
                        dst[c, ghost[side], q, at(i), :] = x + wg * field[0, c, k, q, at(i), :]
        for end in range(2):
            @pl.when(has[end])
            def _():
                for side in range(2):
                    k = rim[side]
                    for q in range(tiles):
                        for c in range(3):
                            x = corner[n, side, end, c, q]
                            a = (c, ghost[side], q, one(edge_row[end]), slice(None))
                            b = (c, k, q, one(beyond[end]), slice(None))
                            dst[a] = dst[a] + w_corner[side, end, q] * x
                            dst[b] = dst[b] + w_face[side, end, q] * x

    red, black0 = field.at[0], field.at[1]

    by_end(stiff_rows, "take")
    inner(lambda k: (make_weights(0, k), make_weights(1, k)))
    by_end(first_rows, "take")
    inner(lambda k: half(0, k, black0, red, red))
    for copy in edge_copies:
        copy.wait_recv()
    for side in range(2):
        for i in range(tile_rows):
            for q in range(tiles):
                x = raw_tile(edge_s, (side,), i, q)
                stiff[0, ghost[side], q, at(i), :] = x
                stiff[1, ghost[side], q, at(i), :] = x
    rims(lambda k: (make_weights(0, k), make_weights(1, k)))
    for copy in g_copies:
        copy.start()
    by_end(scale_rows, "start")
    take_first()
    rims(lambda k: half(0, k, black0, red, red))
    by_end(first_rows, "drain")
    rims(lambda k: half(1, k, red, black0, black0))
    send_theta(0)
    inner(lambda k: half(1, k, red, black0, black0))
    by_end(functools.partial(both_rows, 0), "start")

    by_end(scale_rows, "take")
    rad_weights()
    by_end(functools.partial(both_rows, 0), "take")
    by_end(functools.partial(both_rows, 0), "drain")
    cross_rad(0)
    by_end(functools.partial(red_corners, 0), "drain")
    inner(lambda k: half(0, k, black0, red, red))
    for copy in g_copies:
        copy.wait_recv()
    by_end(edge_corners, "take")
    face_weights()
    for copy in theta_copies(0):
        copy.wait_recv()
    by_end(functools.partial(red_corners, 0), "take")
    cross_theta(0)
    rims(lambda k: half(0, k, black0, red, red))
    rims(lambda k: half(1, k, red, black0, last))
    send_theta(1)
    inner(lambda k: half(1, k, red, black0, last))
    by_end(functools.partial(both_rows, 1), "start")

    def squares(k, acc):
        for i in range(tile_rows):
            for q in range(tiles):
                for c in range(3):
                    change = last[c, k + 1, q, at(i), :] - field[1, c, k + 1, q, at(i), :]
                    acc = acc + change * change
        return acc

    by_end(functools.partial(both_rows, 1), "take")
    by_end(functools.partial(both_rows, 1), "drain")
    cross_rad(1)
    red_sum = lax.fori_loop(1, pairs - 1, lambda k, a: half(0, k, last, red, None, a), zero)
    black_sum = lax.fori_loop(1, pairs - 1, squares, zero)
    for copy in theta_copies(1):
        copy.wait_recv()
    by_end(functools.partial(red_corners, 1), "take")
    cross_theta(1)
    red_sum = lax.fori_loop(0, 2, lambda j, a: half(0, j * (pairs - 1), last, red, None, a), red_sum)
    black_sum = lax.fori_loop(0, 2, lambda j, a: squares(j * (pairs - 1), a), black_sum)

    part[0] = black_sum * (1.0 / 9.0) + red_sum * (1.0 / 2.25)
    for level, peers in enumerate(groups):
        for j, p in enumerate(peers):
            pltpu.make_async_remote_copy(
                part.at[level], gather.at[level, j], ar_send.at[level], ar_recv.at[level], device_id=p, device_id_type=MESH
            ).start()
        if level == 0:
            def unpack(j, _):
                c, k = j // pairs, j % pairs
                for i in range(tile_rows):
                    for q in range(tiles):
                        a, b = field[0, c, k + 1, q, at(i), :], last[c, k + 1, q, at(i), :]
                        x, y = jnp.where(even, a, b), jnp.where(even, b, a)
                        n = LANES if q < tiles - 1 else last_lanes
                        raw_d[c, 2 * k, pl.ds(8 * i, 8), pl.ds(q * LANES, n)] = x[:, :n]
                        raw_d[c, 2 * k + 1, pl.ds(8 * i, 8), pl.ds(q * LANES, n)] = y[:, :n]
                return 0

            lax.fori_loop(0, 3 * pairs, unpack, 0)
            pltpu.make_async_copy(raw_d, out_hbm, out_sem.at[0]).start()
        everything = gather.at[level, pl.ds(0, len(peers))]
        pltpu.make_async_copy(everything, everything, ar_recv.at[level]).wait()
        part[level + 1] = part[level] + jnp.sum(gather[level, : len(peers)], axis=0)
    norm_ref[...] = jnp.sqrt(jnp.sum(part[len(groups)], keepdims=True) / count)

    for level, peers in enumerate(groups):
        everything = gather.at[level, pl.ds(0, len(peers))]
        pltpu.make_async_copy(everything, everything, ar_send.at[level]).wait()
    for copy in edge_copies + first_copies + g_copies + theta_copies(0) + theta_copies(1):
        copy.wait_send()
    for copies in (stiff_rows, edge_corners, scale_rows, functools.partial(red_corners, 1)):
        by_end(copies, "drain")
    pltpu.make_async_copy(raw_d, out_hbm, out_sem.at[0]).wait()


def make_levels(n_theta, n_rad):
    plane = 8 if n_theta % 8 == 0 else n_theta
    stacks = n_theta // plane

    def within(t, r):
        z, x = t // plane, lax.rem(t, plane)
        return [
            (z * plane + lax.rem(x + i, plane), lax.rem(r + j, n_rad))
            for j in range(n_rad) for i in range(plane) if i or j
        ]

    def across(t, r):
        return [(lax.rem(t + i * plane, n_theta), r) for i in range(1, stacks)]

    return (within, across), (n_rad * plane - 1, stacks - 1)


def solution(mesh):
    n_theta, n_rad = mesh.shape["theta"], mesh.shape["rad"]
    levels, sizes = make_levels(n_theta, n_rad)

    def shards(displacement, stiffness, wall):
        planes, rows, cols = stiffness.shape
        pairs, tiles = planes // 2, -(-cols // LANES)
        count = 3.0 * planes * rows * cols * n_theta * n_rad
        cfg = (n_theta, n_rad, pairs, rows, cols, tiles, levels, count)
        dma = pltpu.SemaphoreType.DMA
        moved, norm = pl.pallas_call(
            functools.partial(kernel, cfg),
            out_shape=(jax.ShapeDtypeStruct(displacement.shape, F32), jax.ShapeDtypeStruct((1, 1), F32)),
            in_specs=[pl.BlockSpec(memory_space=pl.ANY)] * 3,
            out_specs=(pl.BlockSpec(memory_space=pl.ANY), pl.BlockSpec(memory_space=pltpu.VMEM)),
            scratch_shapes=[
                pltpu.VMEM((3, planes, rows, cols), F32),
                pltpu.VMEM((planes, rows, cols), F32),
                pltpu.VMEM((planes, rows, cols), jnp.int32),
                pltpu.VMEM((2, 3, pairs + 2, tiles, rows + 16, LANES), F32),
                pltpu.VMEM((3, pairs + 2, tiles, rows + 16, LANES), F32),
                pltpu.VMEM((2, pairs + 2, tiles, rows + 16, LANES), F32),
                pltpu.VMEM((2, 7, pairs, tiles, rows, LANES), F32),
                pltpu.VMEM((pairs, tiles, rows, LANES), F32),
                pltpu.VMEM((2, 3, tiles, rows // 2, LANES), F32),
                pltpu.VMEM((2, 3, tiles, rows // 2, LANES), F32),
                pltpu.VMEM((2, 2, 3, tiles, rows, LANES), F32),
                pltpu.VMEM((2, 2, 3, tiles, rows, LANES), F32),
                pltpu.VMEM((2, tiles, rows, LANES), F32),
                pltpu.VMEM((2, 2, 2, 3, pairs, tiles, 1, LANES), F32),
                pltpu.VMEM((2, pairs, tiles, 1, LANES), F32),
                pltpu.VMEM((2, 2, 2, 3, tiles, 1, LANES), F32),
                pltpu.VMEM((2, rows, cols), F32),
                pltpu.VMEM((2, 2, 1, cols), F32),
                pltpu.VMEM((2, tiles, rows, LANES), F32),
                pltpu.VMEM((2, pairs, tiles, 1, LANES), F32),
                pltpu.VMEM((2, 2, tiles, 1, LANES), F32),
                pltpu.VMEM((2, 2, tiles, 1, LANES), F32),
                pltpu.VMEM((3, 8, LANES), F32),
                pltpu.VMEM((2, max(sizes), 8, LANES), F32),
                dma((3,)), dma((1,)), dma((2,)), dma((2,)), dma((2, 2)), dma((2, 2)), dma((2,)), dma((2,)),
                dma((2,)), dma((2,)), dma((2, 2)), dma((2, 2)), dma((2, 2)), dma((2, 2)), dma((2,)), dma((2,)),
                dma((2, 2, 2)), dma((2, 2, 2)), dma((2,)), dma((2,)), dma((2, 2, 2)), dma((2, 2, 2)), dma((2,)), dma((2,)),
            ],
            compiler_params=pltpu.CompilerParams(collective_id=0, has_side_effects=True, vmem_limit_bytes=60 * 2**20),
            cost_estimate=pl.CostEstimate(flops=10**8, bytes_accessed=4 * 10**6, transcendentals=0),
        )(displacement, stiffness, wall)
        return moved, norm.reshape(())

    placed = (P(None, "theta", "rad", None), P("theta", "rad", None), P("theta", "rad", None))
    return jax.shard_map(
        shards, mesh=mesh, in_specs=placed, out_specs=(P(None, "theta", "rad", None), P()), check_vma=False,
    )
```

```python
import functools

import jax
import jax.numpy as jnp
from jax import lax
from jax.experimental import pallas as pl
from jax.experimental.pallas import tpu as pltpu
from jax.sharding import PartitionSpec as P

MESH = pl.DeviceIdType.MESH
F32 = jnp.float32
LANES = 128
OFF = 8
SELF, IN, OUT, RP, RM, AP, AM = range(7)


def iota(dim):
    return lax.broadcasted_iota(jnp.int32, (8, LANES), dim)


def kernel(
    cfg, d_hbm, s_hbm, w_hbm, out_hbm, norm_ref,
    raw_d, raw_s, raw_w, field, last, stiff, weight, scale_b, first_out, first_in, stage, land, land_g,
    rad_in, rad_g, corner, edge_s, edge_c, w_theta, w_rad, w_face, w_corner, part, gather,
    load_sem, out_sem, f_send, f_recv, t_send, t_recv, g_send, g_recv, es_send, es_recv, ec_send, ec_recv,
    rs_send, rs_recv, r0_send, r0_recv, rd_send, rd_recv, rg_send, rg_recv, c_send, c_recv, ar_send, ar_recv,
):
    n_theta, n_rad, pairs, rows, cols, tiles, levels, count = cfg
    t, r = lax.axis_index("theta"), lax.axis_index("rad")
    tile_rows = rows // 8
    last_lanes = cols - (tiles - 1) * LANES
    t_next, t_prev = lax.rem(t + 1, n_theta), lax.rem(t + n_theta - 1, n_theta)
    r_up, r_down = lax.rem(r + 1, n_rad), lax.rem(r + n_rad - 1, n_rad)
    beside_t = (t_prev, t_next)
    beside_r = (r_down, r_up)
    has = (r > 0, r < n_rad - 1)
    rim = (1, pairs)
    ghost = (0, pairs + 1)
    edge_row = (OFF, OFF + rows - 1)
    beyond = (OFF - 1, OFF + rows)
    own = pl.ds(1, pairs)

    loads = [
        pltpu.make_async_copy(s_hbm, raw_s, load_sem.at[0]),
        pltpu.make_async_copy(d_hbm, raw_d, load_sem.at[1]),
        pltpu.make_async_copy(w_hbm, raw_w, load_sem.at[2]),
    ]
    for c in loads:
        c.start()

    groups = [level(t, r) for level in levels]
    barrier = pltpu.get_barrier_semaphore()
    diagonal = [(tt, rr) for tt in beside_t for rr in beside_r]
    greet = [(tt, r) for tt in beside_t] + diagonal + [p for g in groups for p in g]
    for p in greet:
        pl.semaphore_signal(barrier, inc=1, device_id=p, device_id_type=MESH)

    even = (iota(0) + iota(1)) % 2 == 0
    odd = jnp.logical_not(even)
    lane = lax.broadcasted_iota(jnp.int32, (1, LANES), 1)
    first_lane, last_lane = iota(1) == 0, iota(1) == LANES - 1
    inside = iota(1) < last_lanes
    at_first_col, at_last_col = iota(1) == 0, iota(1) == last_lanes - 1

    def facing(colour, side):
        return even if colour == side else odd

    def raw_tile(ref, lead, i, q):
        if q < tiles - 1:
            return ref[(*lead, pl.ds(8 * i, 8), pl.ds(q * LANES, LANES))]
        x = ref[(*lead, pl.ds(8 * i, 8), pl.ds(q * LANES, last_lanes))]
        if last_lanes == LANES:
            return x
        return jnp.concatenate([x, jnp.zeros((8, LANES - last_lanes), x.dtype)], axis=1)

    def raw_row(ref, lead, q):
        if q < tiles - 1:
            return ref[(*lead, pl.ds(0, 1), pl.ds(q * LANES, LANES))]
        x = ref[(*lead, pl.ds(0, 1), pl.ds(q * LANES, last_lanes))]
        if last_lanes == LANES:
            return x
        return jnp.concatenate([x, jnp.zeros((1, LANES - last_lanes), x.dtype)], axis=1)

    def at(i, shift=0):
        return pl.ds(OFF + 8 * i + shift, 8)

    def one(row):
        return pl.ds(row, 1)

    zero_row = jnp.zeros((1, LANES), F32)
    zero = jnp.zeros((8, LANES), F32)
    loads[0].wait()

    def pack_s(k, _):
        for i in range(tile_rows):
            for q in range(tiles):
                a, b = raw_tile(raw_s, (2 * k,), i, q), raw_tile(raw_s, (2 * k + 1,), i, q)
                stiff[0, k + 1, q, at(i), :] = jnp.where(even, a, b)
                stiff[1, k + 1, q, at(i), :] = jnp.where(even, b, a)
        return 0

    lax.fori_loop(0, pairs, pack_s, 0)
    loads[1].wait()

    def pack_d(j, _):
        c, k = j // pairs, j % pairs
        for i in range(tile_rows):
            for q in range(tiles):
                a, b = raw_tile(raw_d, (c, 2 * k), i, q), raw_tile(raw_d, (c, 2 * k + 1), i, q)
                field[0, c, k + 1, q, at(i), :] = jnp.where(even, a, b)
                field[1, c, k + 1, q, at(i), :] = jnp.where(even, b, a)
        for q in range(tiles):
            for row in beyond:
                field[0, c, k + 1, q, one(row), :] = zero_row
                last[c, k + 1, q, one(row), :] = zero_row
        return 0

    lax.fori_loop(0, 3 * pairs, pack_d, 0)
    for end in range(2):
        @pl.when(jnp.logical_not(has[end]))
        def _():
            def clear(k, _):
                for q in range(tiles):
                    stiff[0, k + 1, q, one(beyond[end]), :] = zero_row
                    stiff[1, k + 1, q, one(beyond[end]), :] = zero_row
                    for c in range(3):
                        field[1, c, k + 1, q, one(beyond[end]), :] = zero_row
                return 0

            lax.fori_loop(0, pairs, clear, 0)

    for c in range(3):
        for g in ghost:
            for q in range(tiles):
                for i in range(tile_rows):
                    field[0, c, g, q, at(i), :] = zero
    loads[2].wait()

    def to(tt, rr):
        return {"device_id": (tt, rr), "device_id_type": MESH}

    def remote(src, dst, send, recv, where):
        return pltpu.make_async_remote_copy(src, dst, send, recv, **where)

    edge_copies = [
        remote(raw_s.at[0 if side == 0 else 2 * pairs - 1], edge_s.at[1 - side], es_send.at[side], es_recv.at[1 - side], to(beside_t[side], r))
        for side in range(2)
    ]
    first_copies = [
        remote(first_out.at[side], first_in.at[1 - side], f_send.at[side], f_recv.at[1 - side], to(beside_t[side], r))
        for side in range(2)
    ]

    def theta_copies(n):
        return [
            remote(stage.at[n, side], land.at[n, 1 - side], t_send.at[n, side], t_recv.at[n, 1 - side], to(beside_t[side], r))
            for side in range(2)
        ]

    g_copies = [
        remote(scale_b.at[rim[side] - 1], land_g.at[1 - side], g_send.at[side], g_recv.at[1 - side], to(beside_t[side], r))
        for side in range(2)
    ]

    def stiff_rows(end):
        return [
            remote(
                stiff.at[colour, own, slice(None), one(edge_row[end])], stiff.at[colour, own, slice(None), one(beyond[1 - end])],
                rs_send.at[colour, end], rs_recv.at[colour, 1 - end], to(t, beside_r[end]),
            )
            for colour in range(2)
        ]

    def edge_corners(end):
        return [
            remote(
                raw_s.at[0 if side == 0 else 2 * pairs - 1, pl.ds(0 if end == 0 else rows - 1, 1)], edge_c.at[1 - side, 1 - end],
                ec_send.at[side, end], ec_recv.at[1 - side, 1 - end], to(beside_t[side], beside_r[end]),
            )
            for side in range(2)
        ]

    def first_rows(end):
        return [
            remote(
                field.at[1, slice(None), own, slice(None), one(edge_row[end])], field.at[1, slice(None), own, slice(None), one(beyond[1 - end])],
                r0_send.at[end], r0_recv.at[1 - end], to(t, beside_r[end]),
            )
        ]

    def black(n):
        return field.at[1] if n == 0 else last

    def both_rows(n, end):
        return [
            remote(
                ref.at[slice(None), own, slice(None), one(edge_row[end])], rad_in.at[n, colour, 1 - end],
                rd_send.at[n, colour, end], rd_recv.at[n, colour, 1 - end], to(t, beside_r[end]),
            )
            for colour, ref in ((0, field.at[0]), (1, black(n)))
        ]

    def scale_rows(end):
        return [
            remote(
                scale_b.at[slice(None), slice(None), one(edge_row[end] - OFF)], rad_g.at[1 - end],
                rg_send.at[end], rg_recv.at[1 - end], to(t, beside_r[end]),
            )
        ]

    def red_corners(n, end):
        return [
            remote(
                field.at[0, slice(None), rim[side], slice(None), one(edge_row[end])], corner.at[n, 1 - side, 1 - end],
                c_send.at[n, side, end], c_recv.at[n, 1 - side, 1 - end], to(beside_t[side], beside_r[end]),
            )
            for side in range(2)
        ]

    def by_end(copies, what):
        for end in range(2):
            @pl.when(has[end])
            def _():
                for copy in copies(end if what != "take" else 1 - end):
                    if what == "start":
                        copy.start()
                    elif what == "take":
                        copy.wait_recv()
                    else:
                        copy.wait_send()

    wide, half_lanes = tiles - 1, LANES // 2
    low = iota(1) < half_lanes

    def put_folded(put, get, n):
        for c in range(3):
            for q in range(wide):
                for i in range(n):
                    put((c * wide + q) * n + i, get(c, q, i))
        for i in range(n):
            put(3 * wide * n + i, jnp.where(low, get(0, wide, i), pltpu.roll(get(1, wide, i), half_lanes, 1)))
        for i in range(n // 2):
            x = pltpu.roll(get(2, wide, i + n // 2), half_lanes, 1)
            put(3 * wide * n + n + i, jnp.where(low, get(2, wide, i), x))

    def get_folded(load, n, c, q, i):
        if q < wide:
            return load((c * wide + q) * n + i)
        if c < 2:
            x = load(3 * wide * n + i)
            return pltpu.roll(x, half_lanes, 1) if c else x
        x = load(3 * wide * n + n + i % (n // 2))
        return x if i < n // 2 else pltpu.roll(x, half_lanes, 1)

    def send_first():
        for side in range(2):
            keep = facing(1, side)

            def get(c, q, h):
                a = field[1, c, rim[side], q, at(2 * h), :]
                b = field[1, c, rim[side], q, at(2 * h + 1), :]
                return jnp.where(keep, a, pltpu.roll(b, 1, 0))

            def put(j, x):
                first_out[side, pl.ds(8 * j, 8), :] = x

            put_folded(put, get, tile_rows // 2)
        for copy in first_copies:
            copy.start()

    def take_first():
        for copy in first_copies:
            copy.wait_recv()
        for side in range(2):
            for c in range(3):
                for q in range(tiles):
                    for h in range(tile_rows // 2):
                        x = get_folded(lambda j: first_in[side, pl.ds(8 * j, 8), :], tile_rows // 2, c, q, h)
                        field[1, c, ghost[side], q, at(2 * h), :] = x
                        field[1, c, ghost[side], q, at(2 * h + 1), :] = pltpu.roll(x, 7, 0)

    def send_theta(n):
        for side in range(2):
            red_here = facing(0, side)

            def get(c, q, i):
                x = field[0, c, rim[side], q, at(i), :]
                y = black(n)[c, rim[side], q, at(i), :]
                return jnp.where(red_here, x, y)

            def put(j, x):
                stage[n, side, pl.ds(8 * j, 8), :] = x

            put_folded(put, get, tile_rows)
        for copy in theta_copies(n):
            copy.start()

    pl.semaphore_wait(barrier, len(greet))
    by_end(edge_corners, "start")
    for copy in edge_copies:
        copy.start()
    send_first()
    by_end(stiff_rows, "start")
    by_end(first_rows, "start")

    def beside(v, side):
        out = []
        for q in range(tiles):
            if side:
                x = pltpu.roll(v[q], LANES - 1, 1)
                if q < tiles - 1:
                    x = jnp.where(last_lane, pltpu.roll(v[q + 1], LANES - 1, 1), x)
            else:
                x = pltpu.roll(v[q], 1, 1)
                if q > 0:
                    x = jnp.where(first_lane, pltpu.roll(v[q - 1], 1, 1), x)
            out.append(x)
        return out

    def outer(colour, before, after):
        return jnp.where(even, before, after) if colour == 0 else jnp.where(even, after, before)

    def make_weights(colour, k):
        other = 1 - colour
        for i in range(tile_rows):
            mid = [stiff[other, k + 1, q, at(i), :] for q in range(tiles)]
            forth, back = beside(mid, 1), beside(mid, 0)
            for q in range(tiles):
                s = stiff[colour, k + 1, q, at(i), :]
                faces = [None] * 7
                faces[IN] = s + mid[q]
                faces[OUT] = s + outer(colour, stiff[other, k, q, at(i), :], stiff[other, k + 2, q, at(i), :])
                faces[RP] = s + stiff[other, k + 1, q, at(i, 1), :]
                faces[RM] = s + stiff[other, k + 1, q, at(i, -1), :]
                ap, am = forth[q], back[q]
                if q == tiles - 1:
                    ap = jnp.where(at_last_col, s, ap)
                if q == 0:
                    am = jnp.where(at_first_col, s, am)
                faces[AP], faces[AM] = s + ap, s + am
                total = faces[IN] + faces[OUT] + (faces[RP] + faces[RM]) + (faces[AP] + faces[AM])
                wa, wb = raw_tile(raw_w, (2 * k,), i, q), raw_tile(raw_w, (2 * k + 1,), i, q)
                fixed = (jnp.where(even, wa, wb) if colour == 0 else jnp.where(even, wb, wa)) != 0
                if q == tiles - 1 and last_lanes < LANES:
                    fixed = jnp.logical_or(fixed, jnp.logical_not(inside))
                scale = jnp.where(fixed, 0.0, 1.5 / total)
                put = pl.ds(8 * i, 8)
                if colour == 1:
                    scale_b[k, q, put, :] = scale
                weight[colour, SELF, k, q, put, :] = jnp.where(fixed, 1.0, -0.5)
                for f in (IN, OUT, RP, RM, AP, AM):
                    w = faces[f] * scale
                    if f == AP and q == tiles - 1:
                        w = jnp.where(at_last_col, 0.0, w)
                    if f == AM and q == 0:
                        w = jnp.where(at_first_col, 0.0, w)
                    weight[colour, f, k, q, put, :] = w

    def half(colour, k, opp, cur, dst, acc=None):
        for i in range(tile_rows):
            put = pl.ds(8 * i, 8)
            w = [[weight[colour, f, k, q, put, :] for q in range(tiles)] for f in range(7)]
            for c in range(3):
                mid = [opp[c, k + 1, q, at(i), :] for q in range(tiles)]
                forth, back = beside(mid, 1), beside(mid, 0)
                for q in range(tiles):
                    far = outer(colour, opp[c, k, q, at(i), :], opp[c, k + 2, q, at(i), :])
                    old = cur[c, k + 1, q, at(i), :]
                    new = w[SELF][q] * old + w[IN][q] * mid[q] + w[OUT][q] * far
                    new = new + w[RP][q] * opp[c, k + 1, q, at(i, 1), :]
                    new = new + w[RM][q] * opp[c, k + 1, q, at(i, -1), :]
                    new = new + w[AP][q] * forth[q] + w[AM][q] * back[q]
                    if dst is not None:
                        dst[c, k + 1, q, at(i), :] = new
                    if acc is not None:
                        change = new - old
                        acc = acc + change * change
        return acc

    def inner(fn):
        lax.fori_loop(1, pairs - 1, lambda k, _: (fn(k), 0)[1], 0)

    def rims(fn):
        lax.fori_loop(0, 2, lambda j, _: (fn(j * (pairs - 1)), 0)[1], 0)

    def face_weights():
        for side in range(2):
            k = rim[side]
            for q in range(tiles):
                for i in range(tile_rows):
                    put = pl.ds(8 * i, 8)
                    w_theta[side, q, put, :] = (stiff[1, ghost[side], q, at(i), :] + stiff[0, k, q, at(i), :]) * land_g[side, q, put, :]
        for end in range(2):
            @pl.when(has[end])
            def _():
                for q in range(tiles):
                    for side in range(2):
                        s = stiff[1, ghost[side], q, one(edge_row[end]), :]
                        g = land_g[side, q, one(edge_row[end] - OFF), :]
                        x = raw_row(edge_c, (side, end), q)
                        w_corner[side, end, q] = (s + x) * g
                        k = rim[side]
                        parity = (beyond[end] + lane) % 2 == 0
                        here = parity if side == 1 else jnp.logical_not(parity)
                        w_face[side, end, q] = jnp.where(here, (stiff[1, k, q, one(beyond[end]), :] + x) * rad_g[end, k - 1, q], 0.0)

    def rad_weights():
        for end in range(2):
            @pl.when(has[end])
            def _():
                def body(k, _):
                    for q in range(tiles):
                        w_rad[end, k, q] = (stiff[1, k + 1, q, one(beyond[end]), :] + stiff[0, k + 1, q, one(edge_row[end]), :]) * rad_g[end, k, q]
                    return 0

                lax.fori_loop(0, pairs, body, 0)

    def cross_rad(n):
        dst = black(n)
        for end in range(2):
            @pl.when(has[end])
            def _():
                f = RP if end else RM

                def body(k, _):
                    for q in range(tiles):
                        w = weight[1, f, k, q, one(edge_row[end] - OFF), :]
                        wg = w_rad[end, k, q]
                        for c in range(3):
                            here = (c, k + 1, q, one(edge_row[end]), slice(None))
                            dst[here] = dst[here] + w * rad_in[n, 0, end, c, k, q]
                            dst[c, k + 1, q, one(beyond[end]), :] = rad_in[n, 1, end, c, k, q] + wg * field[(0, *here)]
                    return 0

                lax.fori_loop(0, pairs, body, 0)

    def cross_theta(n):
        dst = black(n)
        for side in range(2):
            k, here = rim[side], facing(1, side)
            for q in range(tiles):
                for i in range(tile_rows):
                    put = pl.ds(8 * i, 8)
                    w = jnp.where(here, weight[1, OUT, k - 1, q, put, :], 0.0)
                    wg = w_theta[side, q, put, :]
                    for c in range(3):
                        x = get_folded(lambda j: land[n, side, pl.ds(8 * j, 8), :], tile_rows, c, q, i)
                        dst[c, k, q, at(i), :] = dst[c, k, q, at(i), :] + w * x
                        dst[c, ghost[side], q, at(i), :] = x + wg * field[0, c, k, q, at(i), :]
        for end in range(2):
            @pl.when(has[end])
            def _():
                for side in range(2):
                    k = rim[side]
                    for q in range(tiles):
                        for c in range(3):
                            x = corner[n, side, end, c, q]
                            a = (c, ghost[side], q, one(edge_row[end]), slice(None))
                            b = (c, k, q, one(beyond[end]), slice(None))
                            dst[a] = dst[a] + w_corner[side, end, q] * x
                            dst[b] = dst[b] + w_face[side, end, q] * x

    red, black0 = field.at[0], field.at[1]

    by_end(stiff_rows, "take")
    inner(lambda k: (make_weights(0, k), make_weights(1, k)))
    by_end(first_rows, "take")
    inner(lambda k: half(0, k, black0, red, red))
    for copy in edge_copies:
        copy.wait_recv()
    for side in range(2):
        for i in range(tile_rows):
            for q in range(tiles):
                x = raw_tile(edge_s, (side,), i, q)
                stiff[0, ghost[side], q, at(i), :] = x
                stiff[1, ghost[side], q, at(i), :] = x
    rims(lambda k: (make_weights(0, k), make_weights(1, k)))
    for copy in g_copies:
        copy.start()
    by_end(scale_rows, "start")
    take_first()
    rims(lambda k: half(0, k, black0, red, red))
    by_end(functools.partial(red_corners, 0), "start")
    by_end(first_rows, "drain")
    rims(lambda k: half(1, k, red, black0, black0))
    send_theta(0)
    inner(lambda k: half(1, k, red, black0, black0))
    by_end(functools.partial(both_rows, 0), "start")

    by_end(scale_rows, "take")
    rad_weights()
    by_end(functools.partial(both_rows, 0), "take")
    by_end(functools.partial(both_rows, 0), "drain")
    cross_rad(0)
    by_end(functools.partial(red_corners, 0), "drain")
    inner(lambda k: half(0, k, black0, red, red))
    for copy in g_copies:
        copy.wait_recv()
    by_end(edge_corners, "take")
    face_weights()
    for copy in theta_copies(0):
        copy.wait_recv()
    by_end(functools.partial(red_corners, 0), "take")
    cross_theta(0)
    rims(lambda k: half(0, k, black0, red, red))
    by_end(functools.partial(red_corners, 1), "start")
    rims(lambda k: half(1, k, red, black0, last))
    send_theta(1)
    inner(lambda k: half(1, k, red, black0, last))
    by_end(functools.partial(both_rows, 1), "start")

    def squares(k, acc):
        for i in range(tile_rows):
            for q in range(tiles):
                for c in range(3):
                    change = last[c, k + 1, q, at(i), :] - field[1, c, k + 1, q, at(i), :]
                    acc = acc + change * change
        return acc

    by_end(functools.partial(both_rows, 1), "take")
    by_end(functools.partial(both_rows, 1), "drain")
    cross_rad(1)
    red_sum = lax.fori_loop(1, pairs - 1, lambda k, a: half(0, k, last, red, None, a), zero)
    black_sum = lax.fori_loop(1, pairs - 1, squares, zero)
    for copy in theta_copies(1):
        copy.wait_recv()
    by_end(functools.partial(red_corners, 1), "take")
    cross_theta(1)
    red_sum = lax.fori_loop(0, 2, lambda j, a: half(0, j * (pairs - 1), last, red, None, a), red_sum)
    black_sum = lax.fori_loop(0, 2, lambda j, a: squares(j * (pairs - 1), a), black_sum)

    part[0] = jnp.sum(black_sum * (1.0 / 9.0) + red_sum * (1.0 / 2.25), axis=0, keepdims=True)
    for level, peers in enumerate(groups):
        for j, p in enumerate(peers):
            pltpu.make_async_remote_copy(
                part.at[level], gather.at[level, pl.ds(j, 1)], ar_send.at[level], ar_recv.at[level], device_id=p, device_id_type=MESH
            ).start()
        if level == 0:
            def unpack(j, _):
                c, k = j // pairs, j % pairs
                for i in range(tile_rows):
                    for q in range(tiles):
                        a, b = field[0, c, k + 1, q, at(i), :], last[c, k + 1, q, at(i), :]
                        x, y = jnp.where(even, a, b), jnp.where(even, b, a)
                        n = LANES if q < tiles - 1 else last_lanes
                        raw_d[c, 2 * k, pl.ds(8 * i, 8), pl.ds(q * LANES, n)] = x[:, :n]
                        raw_d[c, 2 * k + 1, pl.ds(8 * i, 8), pl.ds(q * LANES, n)] = y[:, :n]
                return 0

            lax.fori_loop(0, 3 * pairs, unpack, 0)
            pltpu.make_async_copy(raw_d, out_hbm, out_sem.at[0]).start()
        everything = gather.at[level, pl.ds(0, len(peers))]
        pltpu.make_async_copy(everything, everything, ar_recv.at[level]).wait()
        part[level + 1] = part[level] + jnp.sum(gather[level, : len(peers)], axis=0, keepdims=True)
    norm_ref[...] = jnp.sqrt(jnp.sum(part[len(groups)], keepdims=True) / count)

    for level, peers in enumerate(groups):
        everything = gather.at[level, pl.ds(0, len(peers))]
        pltpu.make_async_copy(everything, everything, ar_send.at[level]).wait()
    for copy in edge_copies + first_copies + g_copies + theta_copies(0) + theta_copies(1):
        copy.wait_send()
    for copies in (stiff_rows, edge_corners, scale_rows, functools.partial(red_corners, 1)):
        by_end(copies, "drain")
    pltpu.make_async_copy(raw_d, out_hbm, out_sem.at[0]).wait()


def make_levels(n_theta, n_rad):
    plane = 8 if n_theta % 8 == 0 else n_theta
    stacks = n_theta // plane

    def within(t, r):
        z, x = t // plane, lax.rem(t, plane)
        return [
            (z * plane + lax.rem(x + i, plane), lax.rem(r + j, n_rad))
            for j in range(n_rad) for i in range(plane) if i or j
        ]

    def across(t, r):
        return [(lax.rem(t + i * plane, n_theta), r) for i in range(1, stacks)]

    return (within, across), (n_rad * plane - 1, stacks - 1)


def solution(mesh):
    n_theta, n_rad = mesh.shape["theta"], mesh.shape["rad"]
    levels, sizes = make_levels(n_theta, n_rad)

    def shards(displacement, stiffness, wall):
        planes, rows, cols = stiffness.shape
        pairs, tiles = planes // 2, -(-cols // LANES)
        folded = 3 * (tiles - 1) * rows + rows + rows // 2
        count = 3.0 * planes * rows * cols * n_theta * n_rad
        cfg = (n_theta, n_rad, pairs, rows, cols, tiles, levels, count)
        dma = pltpu.SemaphoreType.DMA
        moved, norm = pl.pallas_call(
            functools.partial(kernel, cfg),
            out_shape=(pltpu.VMEM(displacement.shape, F32), jax.ShapeDtypeStruct((1, 1), F32)),
            in_specs=[pl.BlockSpec(memory_space=pl.ANY)] * 3,
            out_specs=(pl.BlockSpec(memory_space=pl.ANY), pl.BlockSpec(memory_space=pltpu.VMEM)),
            scratch_shapes=[
                pltpu.VMEM((3, planes, rows, cols), F32),
                pltpu.VMEM((planes, rows, cols), F32),
                pltpu.VMEM((planes, rows, cols), jnp.int32),
                pltpu.VMEM((2, 3, pairs + 2, tiles, rows + 16, LANES), F32),
                pltpu.VMEM((3, pairs + 2, tiles, rows + 16, LANES), F32),
                pltpu.VMEM((2, pairs + 2, tiles, rows + 16, LANES), F32),
                pltpu.VMEM((2, 7, pairs, tiles, rows, LANES), F32),
                pltpu.VMEM((pairs, tiles, rows, LANES), F32),
                pltpu.VMEM((2, folded // 2, LANES), F32),
                pltpu.VMEM((2, folded // 2, LANES), F32),
                pltpu.VMEM((2, 2, folded, LANES), F32),
                pltpu.VMEM((2, 2, folded, LANES), F32),
                pltpu.VMEM((2, tiles, rows, LANES), F32),
                pltpu.VMEM((2, 2, 2, 3, pairs, tiles, 1, LANES), F32),
                pltpu.VMEM((2, pairs, tiles, 1, LANES), F32),
                pltpu.VMEM((2, 2, 2, 3, tiles, 1, LANES), F32),
                pltpu.VMEM((2, rows, cols), F32),
                pltpu.VMEM((2, 2, 1, cols), F32),
                pltpu.VMEM((2, tiles, rows, LANES), F32),
                pltpu.VMEM((2, pairs, tiles, 1, LANES), F32),
                pltpu.VMEM((2, 2, tiles, 1, LANES), F32),
                pltpu.VMEM((2, 2, tiles, 1, LANES), F32),
                pltpu.VMEM((3, 1, LANES), F32),
                pltpu.VMEM((2, -(-max(sizes) // 8) * 8, LANES), F32),
                dma((3,)), dma((1,)), dma((2,)), dma((2,)), dma((2, 2)), dma((2, 2)), dma((2,)), dma((2,)),
                dma((2,)), dma((2,)), dma((2, 2)), dma((2, 2)), dma((2, 2)), dma((2, 2)), dma((2,)), dma((2,)),
                dma((2, 2, 2)), dma((2, 2, 2)), dma((2,)), dma((2,)), dma((2, 2, 2)), dma((2, 2, 2)), dma((2,)), dma((2,)),
            ],
            compiler_params=pltpu.CompilerParams(collective_id=0, has_side_effects=True, vmem_limit_bytes=56 * 2**20),
            cost_estimate=pl.CostEstimate(flops=10**8, bytes_accessed=4 * 10**6, transcendentals=0),
        )(displacement, stiffness, wall)
        return moved, norm.reshape(())

    placed = (P(None, "theta", "rad", None), P("theta", "rad", None), P("theta", "rad", None))
    return jax.shard_map(
        shards, mesh=mesh, in_specs=placed, out_specs=(P(None, "theta", "rad", None), P()), check_vma=False,
    )
```

```python
import functools

import jax
import jax.numpy as jnp
from jax import lax
from jax.experimental import pallas as pl
from jax.experimental.pallas import tpu as pltpu
from jax.sharding import PartitionSpec as P

MESH = pl.DeviceIdType.MESH
F32 = jnp.float32
LANES = 128
OFF = 8
SELF, IN, OUT, RP, RM, AP, AM = range(7)


def iota(dim):
    return lax.broadcasted_iota(jnp.int32, (8, LANES), dim)


def kernel(
    cfg, d_hbm, s_hbm, w_hbm, out_hbm, norm_ref,
    raw_d, raw_s, raw_w, field, last, stiff, weight, scale_b, first_out, first_in, stage, land, g_out, g_in, land_g,
    rad_in, rad_g, corner, edge_s, edge_c, w_theta, w_rad, w_face, w_corner, part, gather,
    load_sem, out_sem, f_send, f_recv, t_send, t_recv, g_send, g_recv, es_send, es_recv, ec_send, ec_recv,
    rs_send, rs_recv, r0_send, r0_recv, rd_send, rd_recv, rg_send, rg_recv, c_send, c_recv, ar_send, ar_recv,
):
    n_theta, n_rad, pairs, rows, cols, tiles, levels, count = cfg
    t, r = lax.axis_index("theta"), lax.axis_index("rad")
    tile_rows = rows // 8
    last_lanes = cols - (tiles - 1) * LANES
    t_next, t_prev = lax.rem(t + 1, n_theta), lax.rem(t + n_theta - 1, n_theta)
    r_up, r_down = lax.rem(r + 1, n_rad), lax.rem(r + n_rad - 1, n_rad)
    beside_t = (t_prev, t_next)
    beside_r = (r_down, r_up)
    has = (r > 0, r < n_rad - 1)
    rim = (1, pairs)
    ghost = (0, pairs + 1)
    edge_row = (OFF, OFF + rows - 1)
    beyond = (OFF - 1, OFF + rows)
    own = pl.ds(1, pairs)

    groups = [level(t, r) for level in levels]
    barrier = pltpu.get_barrier_semaphore()
    diagonal = [(tt, rr) for tt in beside_t for rr in beside_r]
    greet = diagonal + [(tt, r) for tt in beside_t] + [p for g in reversed(groups) for p in g]
    for p in greet:
        pl.semaphore_signal(barrier, inc=1, device_id=p, device_id_type=MESH)

    rim_loads = [
        pltpu.make_async_copy(d_hbm.at[:, pl.ds(p, 2)], raw_d.at[:, pl.ds(p, 2)], load_sem.at[3 + side])
        for side, p in ((0, 0), (1, 2 * pairs - 2))
    ]
    load_s = pltpu.make_async_copy(s_hbm, raw_s, load_sem.at[0])
    mid = pl.ds(2, 2 * pairs - 4)
    load_d = pltpu.make_async_copy(d_hbm.at[:, mid], raw_d.at[:, mid], load_sem.at[1])
    load_w = pltpu.make_async_copy(w_hbm, raw_w, load_sem.at[2])
    for c in (*rim_loads, load_s, load_d, load_w):
        c.start()

    even = (iota(0) + iota(1)) % 2 == 0
    odd = jnp.logical_not(even)
    lane = lax.broadcasted_iota(jnp.int32, (1, LANES), 1)
    first_lane, last_lane = iota(1) == 0, iota(1) == LANES - 1
    inside = iota(1) < last_lanes
    at_first_col, at_last_col = iota(1) == 0, iota(1) == last_lanes - 1

    def facing(colour, side):
        return even if colour == side else odd

    def raw_tile(ref, lead, i, q):
        if q < tiles - 1:
            return ref[(*lead, pl.ds(8 * i, 8), pl.ds(q * LANES, LANES))]
        x = ref[(*lead, pl.ds(8 * i, 8), pl.ds(q * LANES, last_lanes))]
        if last_lanes == LANES:
            return x
        return jnp.concatenate([x, jnp.zeros((8, LANES - last_lanes), x.dtype)], axis=1)

    def raw_row(ref, lead, q):
        if q < tiles - 1:
            return ref[(*lead, pl.ds(0, 1), pl.ds(q * LANES, LANES))]
        x = ref[(*lead, pl.ds(0, 1), pl.ds(q * LANES, last_lanes))]
        if last_lanes == LANES:
            return x
        return jnp.concatenate([x, jnp.zeros((1, LANES - last_lanes), x.dtype)], axis=1)

    def at(i, shift=0):
        return pl.ds(OFF + 8 * i + shift, 8)

    def one(row):
        return pl.ds(row, 1)

    def to(tt, rr):
        return {"device_id": (tt, rr), "device_id_type": MESH}

    def remote(src, dst, send, recv, where):
        return pltpu.make_async_remote_copy(src, dst, send, recv, **where)

    edge_copies = [
        remote(s_hbm.at[0 if side == 0 else 2 * pairs - 1], edge_s.at[1 - side], es_send.at[side], es_recv.at[1 - side], to(beside_t[side], r))
        for side in range(2)
    ]

    def first_copies(c):
        return [
            remote(first_out.at[side, c], first_in.at[1 - side, c], f_send.at[c, side], f_recv.at[c, 1 - side], to(beside_t[side], r))
            for side in range(2)
        ]

    def theta_copies(n, c):
        return [
            remote(stage.at[n, side, c], land.at[n, 1 - side, c], t_send.at[n, c, side], t_recv.at[n, c, 1 - side], to(beside_t[side], r))
            for side in range(2)
        ]

    g_copies = [
        remote(g_out.at[side], g_in.at[1 - side], g_send.at[side], g_recv.at[1 - side], to(beside_t[side], r))
        for side in range(2)
    ]

    def stiff_rows(end):
        return [
            remote(
                stiff.at[colour, own, slice(None), one(edge_row[end])], stiff.at[colour, own, slice(None), one(beyond[1 - end])],
                rs_send.at[colour, end], rs_recv.at[colour, 1 - end], to(t, beside_r[end]),
            )
            for colour in range(2)
        ]

    def edge_corners(end):
        return [
            remote(
                s_hbm.at[0 if side == 0 else 2 * pairs - 1, pl.ds(0 if end == 0 else rows - 1, 1)], edge_c.at[1 - side, 1 - end],
                ec_send.at[side, end], ec_recv.at[1 - side, 1 - end], to(beside_t[side], beside_r[end]),
            )
            for side in range(2)
        ]

    def first_rows(end):
        return [
            remote(
                field.at[1, slice(None), own, slice(None), one(edge_row[end])], field.at[1, slice(None), own, slice(None), one(beyond[1 - end])],
                r0_send.at[end], r0_recv.at[1 - end], to(t, beside_r[end]),
            )
        ]

    def black(n):
        return field.at[1] if n == 0 else last

    def both_rows(n, end):
        return [
            remote(
                ref.at[slice(None), own, slice(None), one(edge_row[end])], rad_in.at[n, colour, 1 - end],
                rd_send.at[n, colour, end], rd_recv.at[n, colour, 1 - end], to(t, beside_r[end]),
            )
            for colour, ref in ((0, field.at[0]), (1, black(n)))
        ]

    def scale_rows(end):
        return [
            remote(
                scale_b.at[slice(None), slice(None), one(edge_row[end] - OFF)], rad_g.at[1 - end],
                rg_send.at[end], rg_recv.at[1 - end], to(t, beside_r[end]),
            )
        ]

    def red_corners(n, c, end):
        return [
            remote(
                field.at[0, c, rim[side], slice(None), one(edge_row[end])], corner.at[n, 1 - side, 1 - end, c],
                c_send.at[n, c, side, end], c_recv.at[n, c, 1 - side, 1 - end], to(beside_t[side], beside_r[end]),
            )
            for side in range(2)
        ]

    def by_end(copies, what):
        for end in range(2):
            @pl.when(has[end])
            def _():
                for copy in copies(end if what != "take" else 1 - end):
                    if what == "start":
                        copy.start()
                    elif what == "take":
                        copy.wait_recv()
                    else:
                        copy.wait_send()

    wide, half_lanes = tiles - 1, LANES // 2
    low = iota(1) < half_lanes

    def put_folded(put, get, n):
        for q in range(wide):
            for i in range(n):
                put(q * n + i, get(q, i))
        for i in range(n // 2):
            put(wide * n + i, jnp.where(low, get(wide, i), pltpu.roll(get(wide, i + n // 2), half_lanes, 1)))

    def get_folded(load, n, q, i):
        if q < wide:
            return load(q * n + i)
        x = load(wide * n + i % (n // 2))
        return x if i < n // 2 else pltpu.roll(x, half_lanes, 1)

    def pack_first(c):
        for side in range(2):
            keep = facing(1, side)

            def get(q, h):
                a = field[1, c, rim[side], q, at(2 * h), :]
                b = field[1, c, rim[side], q, at(2 * h + 1), :]
                return jnp.where(keep, a, pltpu.roll(b, 1, 0))

            def put(j, x):
                first_out[side, c, pl.ds(8 * j, 8), :] = x

            put_folded(put, get, tile_rows // 2)

    def pack_g():
        for side in range(2):
            keep = facing(1, side)

            def get(q, h):
                a = scale_b[rim[side] - 1, q, pl.ds(16 * h, 8), :]
                b = scale_b[rim[side] - 1, q, pl.ds(16 * h + 8, 8), :]
                return jnp.where(keep, a, pltpu.roll(b, 1, 0))

            def put(j, x):
                g_out[side, pl.ds(8 * j, 8), :] = x

            put_folded(put, get, tile_rows // 2)

    def take_g():
        for side in range(2):
            for q in range(tiles):
                for h in range(tile_rows // 2):
                    x = get_folded(lambda j: g_in[side, pl.ds(8 * j, 8), :], tile_rows // 2, q, h)
                    land_g[side, q, pl.ds(16 * h, 8), :] = x
                    land_g[side, q, pl.ds(16 * h + 8, 8), :] = pltpu.roll(x, 7, 0)

    def take_first(c):
        for copy in first_copies(c):
            copy.wait_recv()
        for side in range(2):
            for q in range(tiles):
                for h in range(tile_rows // 2):
                    x = get_folded(lambda j: first_in[side, c, pl.ds(8 * j, 8), :], tile_rows // 2, q, h)
                    field[1, c, ghost[side], q, at(2 * h), :] = x
                    field[1, c, ghost[side], q, at(2 * h + 1), :] = pltpu.roll(x, 7, 0)

    def send_theta(n, c):
        for side in range(2):
            red_here = facing(0, side)

            def get(q, i):
                x = field[0, c, rim[side], q, at(i), :]
                y = black(n)[c, rim[side], q, at(i), :]
                return jnp.where(red_here, x, y)

            def put(j, x):
                stage[n, side, c, pl.ds(8 * j, 8), :] = x

            put_folded(put, get, tile_rows)
        for copy in theta_copies(n, c):
            copy.start()

    zero_row = jnp.zeros((1, LANES), F32)
    zero = jnp.zeros((8, LANES), F32)

    def pack_s(k, _):
        for i in range(tile_rows):
            for q in range(tiles):
                a, b = raw_tile(raw_s, (2 * k,), i, q), raw_tile(raw_s, (2 * k + 1,), i, q)
                stiff[0, k + 1, q, at(i), :] = jnp.where(even, a, b)
                stiff[1, k + 1, q, at(i), :] = jnp.where(even, b, a)
        return 0

    def pack_d(k, _):
        for c in range(3):
            for i in range(tile_rows):
                for q in range(tiles):
                    a, b = raw_tile(raw_d, (c, 2 * k), i, q), raw_tile(raw_d, (c, 2 * k + 1), i, q)
                    field[0, c, k + 1, q, at(i), :] = jnp.where(even, a, b)
                    field[1, c, k + 1, q, at(i), :] = jnp.where(even, b, a)
        return 0

    def clear_rows(k, _):
        for c in range(3):
            for q in range(tiles):
                for row in beyond:
                    field[0, c, k + 1, q, one(row), :] = zero_row
                    last[c, k + 1, q, one(row), :] = zero_row
        return 0

    for c in rim_loads:
        c.wait()
    lax.fori_loop(0, 2, lambda j, _: pack_d(j * (pairs - 1), 0), 0)
    for c in range(3):
        pack_first(c)
    pl.semaphore_wait(barrier, len(greet))
    by_end(edge_corners, "start")
    for copy in edge_copies + [x for c in range(3) for x in first_copies(c)]:
        copy.start()
    load_s.wait()
    lax.fori_loop(0, pairs, pack_s, 0)
    by_end(stiff_rows, "start")
    load_d.wait()
    lax.fori_loop(1, pairs - 1, pack_d, 0)
    by_end(first_rows, "start")
    lax.fori_loop(0, pairs, clear_rows, 0)
    for end in range(2):
        @pl.when(jnp.logical_not(has[end]))
        def _():
            def clear(k, _):
                for q in range(tiles):
                    stiff[0, k + 1, q, one(beyond[end]), :] = zero_row
                    stiff[1, k + 1, q, one(beyond[end]), :] = zero_row
                    for c in range(3):
                        field[1, c, k + 1, q, one(beyond[end]), :] = zero_row
                return 0

            lax.fori_loop(0, pairs, clear, 0)
            for side in range(2):
                for q in range(tiles):
                    w_corner[side, end, q] = zero_row
                    w_face[side, end, q] = zero_row
                    for n in range(2):
                        for c in range(3):
                            corner[n, side, end, c, q] = zero_row

    for c in range(3):
        for g in ghost:
            for q in range(tiles):
                for i in range(tile_rows):
                    field[0, c, g, q, at(i), :] = zero
    load_w.wait()

    def beside(v, side):
        out = []
        for q in range(tiles):
            if side:
                x = pltpu.roll(v[q], LANES - 1, 1)
                if q < tiles - 1:
                    x = jnp.where(last_lane, pltpu.roll(v[q + 1], LANES - 1, 1), x)
            else:
                x = pltpu.roll(v[q], 1, 1)
                if q > 0:
                    x = jnp.where(first_lane, pltpu.roll(v[q - 1], 1, 1), x)
            out.append(x)
        return out

    def outer(colour, before, after):
        return jnp.where(even, before, after) if colour == 0 else jnp.where(even, after, before)

    def make_weights(colour, k):
        other = 1 - colour
        for i in range(tile_rows):
            mid = [stiff[other, k + 1, q, at(i), :] for q in range(tiles)]
            forth, back = beside(mid, 1), beside(mid, 0)
            for q in range(tiles):
                s = stiff[colour, k + 1, q, at(i), :]
                faces = [None] * 7
                faces[IN] = s + mid[q]
                faces[OUT] = s + outer(colour, stiff[other, k, q, at(i), :], stiff[other, k + 2, q, at(i), :])
                faces[RP] = s + stiff[other, k + 1, q, at(i, 1), :]
                faces[RM] = s + stiff[other, k + 1, q, at(i, -1), :]
                ap, am = forth[q], back[q]
                if q == tiles - 1:
                    ap = jnp.where(at_last_col, s, ap)
                if q == 0:
                    am = jnp.where(at_first_col, s, am)
                faces[AP], faces[AM] = s + ap, s + am
                total = faces[IN] + faces[OUT] + (faces[RP] + faces[RM]) + (faces[AP] + faces[AM])
                wa, wb = raw_tile(raw_w, (2 * k,), i, q), raw_tile(raw_w, (2 * k + 1,), i, q)
                fixed = (jnp.where(even, wa, wb) if colour == 0 else jnp.where(even, wb, wa)) != 0
                if q == tiles - 1 and last_lanes < LANES:
                    fixed = jnp.logical_or(fixed, jnp.logical_not(inside))
                scale = jnp.where(fixed, 0.0, 1.5 / total)
                put = pl.ds(8 * i, 8)
                if colour == 1:
                    scale_b[k, q, put, :] = scale
                weight[colour, SELF, k, q, put, :] = jnp.where(fixed, 1.0, -0.5)
                for f in (IN, OUT, RP, RM, AP, AM):
                    w = faces[f] * scale
                    if f == AP and q == tiles - 1:
                        w = jnp.where(at_last_col, 0.0, w)
                    if f == AM and q == 0:
                        w = jnp.where(at_first_col, 0.0, w)
                    weight[colour, f, k, q, put, :] = w

    def half(colour, k, opp, cur, dst, acc=None, comps=range(3)):
        for i in range(tile_rows):
            put = pl.ds(8 * i, 8)
            w = [[weight[colour, f, k, q, put, :] for q in range(tiles)] for f in range(7)]
            for c in comps:
                mid = [opp[c, k + 1, q, at(i), :] for q in range(tiles)]
                forth, back = beside(mid, 1), beside(mid, 0)
                for q in range(tiles):
                    far = outer(colour, opp[c, k, q, at(i), :], opp[c, k + 2, q, at(i), :])
                    old = cur[c, k + 1, q, at(i), :]
                    new = w[SELF][q] * old + w[IN][q] * mid[q] + w[OUT][q] * far
                    new = new + w[RP][q] * opp[c, k + 1, q, at(i, 1), :]
                    new = new + w[RM][q] * opp[c, k + 1, q, at(i, -1), :]
                    new = new + w[AP][q] * forth[q] + w[AM][q] * back[q]
                    if dst is not None:
                        dst[c, k + 1, q, at(i), :] = new
                    if acc is not None:
                        change = new - old
                        acc = acc + change * change
        return acc

    def inner(fn):
        lax.fori_loop(1, pairs - 1, lambda k, _: (fn(k), 0)[1], 0)

    def rims(fn):
        for k in (0, pairs - 1):
            fn(k)

    def face_weights():
        for side in range(2):
            k = rim[side]
            for q in range(tiles):
                for i in range(tile_rows):
                    put = pl.ds(8 * i, 8)
                    w_theta[side, q, put, :] = (stiff[1, ghost[side], q, at(i), :] + stiff[0, k, q, at(i), :]) * land_g[side, q, put, :]
        for end in range(2):
            @pl.when(has[end])
            def _():
                for q in range(tiles):
                    for side in range(2):
                        s = stiff[1, ghost[side], q, one(edge_row[end]), :]
                        g = land_g[side, q, one(edge_row[end] - OFF), :]
                        x = raw_row(edge_c, (side, end), q)
                        w_corner[side, end, q] = (s + x) * g
                        k = rim[side]
                        parity = (beyond[end] + lane) % 2 == 0
                        here = parity if side == 1 else jnp.logical_not(parity)
                        w_face[side, end, q] = jnp.where(here, (stiff[1, k, q, one(beyond[end]), :] + x) * rad_g[end, k - 1, q], 0.0)

    def rad_weights():
        for end in range(2):
            @pl.when(has[end])
            def _():
                def body(k, _):
                    for q in range(tiles):
                        w_rad[end, k, q] = (stiff[1, k + 1, q, one(beyond[end]), :] + stiff[0, k + 1, q, one(edge_row[end]), :]) * rad_g[end, k, q]
                    return 0

                lax.fori_loop(0, pairs, body, 0)

    def cross_rad(n):
        dst = black(n)
        for end in range(2):
            @pl.when(has[end])
            def _():
                f = RP if end else RM

                def body(k, _):
                    for q in range(tiles):
                        w = weight[1, f, k, q, one(edge_row[end] - OFF), :]
                        wg = w_rad[end, k, q]
                        for c in range(3):
                            here = (c, k + 1, q, one(edge_row[end]), slice(None))
                            dst[here] = dst[here] + w * rad_in[n, 0, end, c, k, q]
                            dst[c, k + 1, q, one(beyond[end]), :] = rad_in[n, 1, end, c, k, q] + wg * field[(0, *here)]
                    return 0

                lax.fori_loop(0, pairs, body, 0)

    def cross_theta(n, c):
        dst = black(n)
        for side in range(2):
            k, here = rim[side], facing(1, side)
            for q in range(tiles):
                for i in range(tile_rows):
                    put = pl.ds(8 * i, 8)
                    w = jnp.where(here, weight[1, OUT, k - 1, q, put, :], 0.0)
                    wg = w_theta[side, q, put, :]
                    x = get_folded(lambda j: land[n, side, c, pl.ds(8 * j, 8), :], tile_rows, q, i)
                    dst[c, k, q, at(i), :] = dst[c, k, q, at(i), :] + w * x
                    dst[c, ghost[side], q, at(i), :] = x + wg * field[0, c, k, q, at(i), :]
        for end in range(2):
            for side in range(2):
                for q in range(tiles):
                    x = corner[n, side, end, c, q]
                    a = (c, ghost[side], q, one(edge_row[end]), slice(None))
                    b = (c, rim[side], q, one(beyond[end]), slice(None))
                    dst[a] = dst[a] + w_corner[side, end, q] * x
                    dst[b] = dst[b] + w_face[side, end, q] * x

    red, black0 = field.at[0], field.at[1]

    by_end(stiff_rows, "take")
    inner(lambda k: (make_weights(0, k), make_weights(1, k)))
    by_end(first_rows, "take")
    inner(lambda k: half(0, k, black0, red, red))
    for copy in edge_copies:
        copy.wait_recv()
    for side in range(2):
        for i in range(tile_rows):
            for q in range(tiles):
                x = raw_tile(edge_s, (side,), i, q)
                stiff[0, ghost[side], q, at(i), :] = x
                stiff[1, ghost[side], q, at(i), :] = x
    rims(lambda k: (make_weights(0, k), make_weights(1, k)))
    pack_g()
    for copy in g_copies:
        copy.start()
    by_end(scale_rows, "start")
    by_end(first_rows, "drain")
    for c in range(3):
        take_first(c)
        rims(lambda k: half(0, k, black0, red, red, comps=(c,)))
        by_end(functools.partial(red_corners, 0, c), "start")
        rims(lambda k: half(1, k, red, black0, black0, comps=(c,)))
        send_theta(0, c)
    inner(lambda k: half(1, k, red, black0, black0))
    by_end(functools.partial(both_rows, 0), "start")

    by_end(scale_rows, "take")
    rad_weights()
    by_end(functools.partial(both_rows, 0), "take")
    by_end(functools.partial(both_rows, 0), "drain")
    cross_rad(0)
    for c in range(3):
        by_end(functools.partial(red_corners, 0, c), "drain")
    inner(lambda k: half(0, k, black0, red, red))
    for copy in g_copies:
        copy.wait_recv()
    take_g()
    by_end(edge_corners, "take")
    face_weights()
    for c in range(3):
        for copy in theta_copies(0, c):
            copy.wait_recv()
        by_end(functools.partial(red_corners, 0, c), "take")
        cross_theta(0, c)
        rims(lambda k: half(0, k, black0, red, red, comps=(c,)))
        by_end(functools.partial(red_corners, 1, c), "start")
        rims(lambda k: half(1, k, red, black0, last, comps=(c,)))
        send_theta(1, c)
    inner(lambda k: half(1, k, red, black0, last))
    by_end(functools.partial(both_rows, 1), "start")

    def squares(k, acc, comps=range(3)):
        for i in range(tile_rows):
            for q in range(tiles):
                for c in comps:
                    change = last[c, k + 1, q, at(i), :] - field[1, c, k + 1, q, at(i), :]
                    acc = acc + change * change
        return acc

    by_end(functools.partial(both_rows, 1), "take")
    by_end(functools.partial(both_rows, 1), "drain")
    cross_rad(1)
    red_sum = lax.fori_loop(1, pairs - 1, lambda k, a: half(0, k, last, red, None, a), zero)
    black_sum = lax.fori_loop(1, pairs - 1, squares, zero)
    for c in range(3):
        for copy in theta_copies(1, c):
            copy.wait_recv()
        by_end(functools.partial(red_corners, 1, c), "take")
        cross_theta(1, c)
        for k in (0, pairs - 1):
            red_sum = half(0, k, last, red, None, red_sum, comps=(c,))
            black_sum = squares(k, black_sum, comps=(c,))

    part[0] = jnp.sum(black_sum * (1.0 / 9.0) + red_sum * (1.0 / 2.25), axis=0, keepdims=True)
    for level, peers in enumerate(groups):
        for j, p in enumerate(peers):
            pltpu.make_async_remote_copy(
                part.at[level], gather.at[level, pl.ds(j, 1)], ar_send.at[level], ar_recv.at[level], device_id=p, device_id_type=MESH
            ).start()
        if level == 0:
            def unpack(j, _):
                c, k = j // pairs, j % pairs
                for i in range(tile_rows):
                    for q in range(tiles):
                        a, b = field[0, c, k + 1, q, at(i), :], last[c, k + 1, q, at(i), :]
                        x, y = jnp.where(even, a, b), jnp.where(even, b, a)
                        n = LANES if q < tiles - 1 else last_lanes
                        raw_d[c, 2 * k, pl.ds(8 * i, 8), pl.ds(q * LANES, n)] = x[:, :n]
                        raw_d[c, 2 * k + 1, pl.ds(8 * i, 8), pl.ds(q * LANES, n)] = y[:, :n]
                return 0

            lax.fori_loop(0, 3 * pairs, unpack, 0)
            pltpu.make_async_copy(raw_d, out_hbm, out_sem.at[0]).start()
        everything = gather.at[level, pl.ds(0, len(peers))]
        pltpu.make_async_copy(everything, everything, ar_recv.at[level]).wait()
        part[level + 1] = part[level] + jnp.sum(gather[level, : len(peers)], axis=0, keepdims=True)
    norm_ref[...] = jnp.sqrt(jnp.sum(part[len(groups)], keepdims=True) / count)

    for level, peers in enumerate(groups):
        everything = gather.at[level, pl.ds(0, len(peers))]
        pltpu.make_async_copy(everything, everything, ar_send.at[level]).wait()
    for copy in edge_copies + g_copies + [x for c in range(3) for x in first_copies(c) + theta_copies(0, c) + theta_copies(1, c)]:
        copy.wait_send()
    for copies in (stiff_rows, edge_corners, scale_rows, *(functools.partial(red_corners, 1, c) for c in range(3))):
        by_end(copies, "drain")
    pltpu.make_async_copy(raw_d, out_hbm, out_sem.at[0]).wait()


def make_levels(n_theta, n_rad):
    plane = 8 if n_theta % 8 == 0 else n_theta
    stacks = n_theta // plane

    def within(t, r):
        z, x = t // plane, lax.rem(t, plane)
        return [
            (z * plane + lax.rem(x + i, plane), lax.rem(r + j, n_rad))
            for j in range(n_rad) for i in range(plane) if i or j
        ]

    def across(t, r):
        return [(lax.rem(t + i * plane, n_theta), r) for i in range(1, stacks)]

    return (within, across), (n_rad * plane - 1, stacks - 1)


def solution(mesh):
    n_theta, n_rad = mesh.shape["theta"], mesh.shape["rad"]
    levels, sizes = make_levels(n_theta, n_rad)

    def shards(displacement, stiffness, wall):
        planes, rows, cols = stiffness.shape
        pairs, tiles = planes // 2, -(-cols // LANES)
        folded = (tiles - 1) * rows + rows // 2
        count = 3.0 * planes * rows * cols * n_theta * n_rad
        cfg = (n_theta, n_rad, pairs, rows, cols, tiles, levels, count)
        dma = pltpu.SemaphoreType.DMA
        moved, norm = pl.pallas_call(
            functools.partial(kernel, cfg),
            out_shape=(pltpu.VMEM(displacement.shape, F32), jax.ShapeDtypeStruct((1, 1), F32)),
            in_specs=[pl.BlockSpec(memory_space=pl.ANY)] * 3,
            out_specs=(pl.BlockSpec(memory_space=pl.ANY), pl.BlockSpec(memory_space=pltpu.VMEM)),
            scratch_shapes=[
                pltpu.VMEM((3, planes, rows, cols), F32),
                pltpu.VMEM((planes, rows, cols), F32),
                pltpu.VMEM((planes, rows, cols), jnp.int32),
                pltpu.VMEM((2, 3, pairs + 2, tiles, rows + 16, LANES), F32),
                pltpu.VMEM((3, pairs + 2, tiles, rows + 16, LANES), F32),
                pltpu.VMEM((2, pairs + 2, tiles, rows + 16, LANES), F32),
                pltpu.VMEM((2, 7, pairs, tiles, rows, LANES), F32),
                pltpu.VMEM((pairs, tiles, rows, LANES), F32),
                pltpu.VMEM((2, 3, folded // 2, LANES), F32),
                pltpu.VMEM((2, 3, folded // 2, LANES), F32),
                pltpu.VMEM((2, 2, 3, folded, LANES), F32),
                pltpu.VMEM((2, 2, 3, folded, LANES), F32),
                pltpu.VMEM((2, folded // 2, LANES), F32),
                pltpu.VMEM((2, folded // 2, LANES), F32),
                pltpu.VMEM((2, tiles, rows, LANES), F32),
                pltpu.VMEM((2, 2, 2, 3, pairs, tiles, 1, LANES), F32),
                pltpu.VMEM((2, pairs, tiles, 1, LANES), F32),
                pltpu.VMEM((2, 2, 2, 3, tiles, 1, LANES), F32),
                pltpu.VMEM((2, rows, cols), F32),
                pltpu.VMEM((2, 2, 1, cols), F32),
                pltpu.VMEM((2, tiles, rows, LANES), F32),
                pltpu.VMEM((2, pairs, tiles, 1, LANES), F32),
                pltpu.VMEM((2, 2, tiles, 1, LANES), F32),
                pltpu.VMEM((2, 2, tiles, 1, LANES), F32),
                pltpu.VMEM((3, 1, LANES), F32),
                pltpu.VMEM((2, -(-max(sizes) // 8) * 8, LANES), F32),
                dma((5,)), dma((1,)), dma((3, 2)), dma((3, 2)), dma((2, 3, 2)), dma((2, 3, 2)), dma((2,)), dma((2,)),
                dma((2,)), dma((2,)), dma((2, 2)), dma((2, 2)), dma((2, 2)), dma((2, 2)), dma((2,)), dma((2,)),
                dma((2, 2, 2)), dma((2, 2, 2)), dma((2,)), dma((2,)), dma((2, 3, 2, 2)), dma((2, 3, 2, 2)), dma((2,)), dma((2,)),
            ],
            compiler_params=pltpu.CompilerParams(collective_id=0, has_side_effects=True, vmem_limit_bytes=56 * 2**20),
            cost_estimate=pl.CostEstimate(flops=10**8, bytes_accessed=4 * 10**6, transcendentals=0),
        )(displacement, stiffness, wall)
        return moved, norm.reshape(())

    placed = (P(None, "theta", "rad", None), P("theta", "rad", None), P("theta", "rad", None))
    return jax.shard_map(
        shards, mesh=mesh, in_specs=placed, out_specs=(P(None, "theta", "rad", None), P()), check_vma=False,
    )
```

```python
import functools

import jax
import jax.numpy as jnp
from jax import lax
from jax.experimental import pallas as pl
from jax.experimental.pallas import tpu as pltpu
from jax.sharding import PartitionSpec as P

MESH = pl.DeviceIdType.MESH
F32 = jnp.float32
LANES = 128
OFF = 8
SELF, IN, OUT, RP, RM, AP, AM = range(7)


def iota(dim):
    return lax.broadcasted_iota(jnp.int32, (8, LANES), dim)


def kernel(
    cfg, d_hbm, s_hbm, w_hbm, out_hbm, norm_ref,
    raw_d, raw_s, raw_w, field, last, stiff, weight, scale_b, first_out, first_in, stage, land, g_out, g_in, land_g,
    rad_in, rad_g, corner, edge_s, edge_c, w_theta, w_rad, w_face, w_corner, part, gather,
    load_sem, out_sem, f_send, f_recv, t_send, t_recv, g_send, g_recv, es_send, es_recv, ec_send, ec_recv,
    rs_send, rs_recv, r0_send, r0_recv, rd_send, rd_recv, rg_send, rg_recv, c_send, c_recv, ar_send, ar_recv,
):
    n_theta, n_rad, pairs, rows, cols, tiles, levels, count = cfg
    t, r = lax.axis_index("theta"), lax.axis_index("rad")
    tile_rows = rows // 8
    last_lanes = cols - (tiles - 1) * LANES
    t_next, t_prev = lax.rem(t + 1, n_theta), lax.rem(t + n_theta - 1, n_theta)
    r_up, r_down = lax.rem(r + 1, n_rad), lax.rem(r + n_rad - 1, n_rad)
    beside_t = (t_prev, t_next)
    beside_r = (r_down, r_up)
    has = (r > 0, r < n_rad - 1)
    rim = (1, pairs)
    ghost = (0, pairs + 1)
    edge_row = (OFF, OFF + rows - 1)
    beyond = (OFF - 1, OFF + rows)
    own = pl.ds(1, pairs)

    groups = [level(t, r) for level in levels]
    barrier = pltpu.get_barrier_semaphore()
    diagonal = [(tt, rr) for tt in beside_t for rr in beside_r]
    greet = diagonal + [(tt, r) for tt in beside_t] + [p for g in reversed(groups) for p in g]
    for p in greet:
        pl.semaphore_signal(barrier, inc=1, device_id=p, device_id_type=MESH)

    rim_loads = [
        pltpu.make_async_copy(d_hbm.at[:, pl.ds(p, 2)], raw_d.at[:, pl.ds(p, 2)], load_sem.at[3 + side])
        for side, p in ((0, 0), (1, 2 * pairs - 2))
    ]
    load_s = pltpu.make_async_copy(s_hbm, raw_s, load_sem.at[0])
    mid = pl.ds(2, 2 * pairs - 4)
    load_d = pltpu.make_async_copy(d_hbm.at[:, mid], raw_d.at[:, mid], load_sem.at[1])
    load_w = pltpu.make_async_copy(w_hbm, raw_w, load_sem.at[2])
    for c in (*rim_loads, load_s, load_d, load_w):
        c.start()

    even = (iota(0) + iota(1)) % 2 == 0
    odd = jnp.logical_not(even)
    lane = lax.broadcasted_iota(jnp.int32, (1, LANES), 1)
    first_lane, last_lane = iota(1) == 0, iota(1) == LANES - 1
    inside = iota(1) < last_lanes
    at_first_col, at_last_col = iota(1) == 0, iota(1) == last_lanes - 1

    def facing(colour, side):
        return even if colour == side else odd

    def raw_tile(ref, lead, i, q):
        if q < tiles - 1:
            return ref[(*lead, pl.ds(8 * i, 8), pl.ds(q * LANES, LANES))]
        x = ref[(*lead, pl.ds(8 * i, 8), pl.ds(q * LANES, last_lanes))]
        if last_lanes == LANES:
            return x
        return jnp.concatenate([x, jnp.zeros((8, LANES - last_lanes), x.dtype)], axis=1)

    def raw_row(ref, lead, q):
        if q < tiles - 1:
            return ref[(*lead, pl.ds(0, 1), pl.ds(q * LANES, LANES))]
        x = ref[(*lead, pl.ds(0, 1), pl.ds(q * LANES, last_lanes))]
        if last_lanes == LANES:
            return x
        return jnp.concatenate([x, jnp.zeros((1, LANES - last_lanes), x.dtype)], axis=1)

    def at(i, shift=0):
        return pl.ds(OFF + 8 * i + shift, 8)

    def one(row):
        return pl.ds(row, 1)

    def to(tt, rr):
        return {"device_id": (tt, rr), "device_id_type": MESH}

    def remote(src, dst, send, recv, where):
        return pltpu.make_async_remote_copy(src, dst, send, recv, **where)

    edge_copies = [
        remote(s_hbm.at[0 if side == 0 else 2 * pairs - 1], edge_s.at[1 - side], es_send.at[side], es_recv.at[1 - side], to(beside_t[side], r))
        for side in range(2)
    ]

    def first_copies(c):
        return [
            remote(first_out.at[side, c], first_in.at[1 - side, c], f_send.at[c, side], f_recv.at[c, 1 - side], to(beside_t[side], r))
            for side in range(2)
        ]

    def theta_copies(n, c):
        return [
            remote(stage.at[n, side, c], land.at[n, 1 - side, c], t_send.at[n, c, side], t_recv.at[n, c, 1 - side], to(beside_t[side], r))
            for side in range(2)
        ]

    g_copies = [
        remote(g_out.at[side], g_in.at[1 - side], g_send.at[side], g_recv.at[1 - side], to(beside_t[side], r))
        for side in range(2)
    ]

    def stiff_rows(end):
        return [
            remote(
                stiff.at[colour, own, slice(None), one(edge_row[end])], stiff.at[colour, own, slice(None), one(beyond[1 - end])],
                rs_send.at[colour, end], rs_recv.at[colour, 1 - end], to(t, beside_r[end]),
            )
            for colour in range(2)
        ]

    def edge_corners(end):
        return [
            remote(
                s_hbm.at[0 if side == 0 else 2 * pairs - 1, pl.ds(0 if end == 0 else rows - 1, 1)], edge_c.at[1 - side, 1 - end],
                ec_send.at[side, end], ec_recv.at[1 - side, 1 - end], to(beside_t[side], beside_r[end]),
            )
            for side in range(2)
        ]

    def first_rows(end):
        return [
            remote(
                field.at[1, slice(None), own, slice(None), one(edge_row[end])], field.at[1, slice(None), own, slice(None), one(beyond[1 - end])],
                r0_send.at[end], r0_recv.at[1 - end], to(t, beside_r[end]),
            )
        ]

    def black(n):
        return field.at[1] if n == 0 else last

    def both_rows(n, end):
        return [
            remote(
                ref.at[slice(None), own, slice(None), one(edge_row[end])], rad_in.at[n, colour, 1 - end],
                rd_send.at[n, colour, end], rd_recv.at[n, colour, 1 - end], to(t, beside_r[end]),
            )
            for colour, ref in ((0, field.at[0]), (1, black(n)))
        ]

    def scale_rows(end):
        return [
            remote(
                scale_b.at[slice(None), slice(None), one(edge_row[end] - OFF)], rad_g.at[1 - end],
                rg_send.at[end], rg_recv.at[1 - end], to(t, beside_r[end]),
            )
        ]

    def red_corners(n, c, end):
        return [
            remote(
                field.at[0, c, rim[side], slice(None), one(edge_row[end])], corner.at[n, 1 - side, 1 - end, c],
                c_send.at[n, c, side, end], c_recv.at[n, c, 1 - side, 1 - end], to(beside_t[side], beside_r[end]),
            )
            for side in range(2)
        ]

    def by_end(copies, what):
        for end in range(2):
            @pl.when(has[end])
            def _():
                for copy in copies(end if what != "take" else 1 - end):
                    if what == "start":
                        copy.start()
                    elif what == "take":
                        copy.wait_recv()
                    else:
                        copy.wait_send()

    wide, half_lanes = tiles - 1, LANES // 2
    low = iota(1) < half_lanes

    def put_folded(put, get, n):
        for q in range(wide):
            for i in range(n):
                put(q * n + i, get(q, i))
        for i in range(n // 2):
            put(wide * n + i, jnp.where(low, get(wide, i), pltpu.roll(get(wide, i + n // 2), half_lanes, 1)))

    def get_folded(load, n, q, i):
        if q < wide:
            return load(q * n + i)
        x = load(wide * n + i % (n // 2))
        return x if i < n // 2 else pltpu.roll(x, half_lanes, 1)

    def pack_first(c):
        for side in range(2):
            keep = facing(1, side)

            def get(q, h):
                a = field[1, c, rim[side], q, at(2 * h), :]
                b = field[1, c, rim[side], q, at(2 * h + 1), :]
                return jnp.where(keep, a, pltpu.roll(b, 1, 0))

            def put(j, x):
                first_out[side, c, pl.ds(8 * j, 8), :] = x

            put_folded(put, get, tile_rows // 2)

    def pack_g():
        for side in range(2):
            keep = facing(1, side)

            def get(q, h):
                a = scale_b[rim[side] - 1, q, pl.ds(16 * h, 8), :]
                b = scale_b[rim[side] - 1, q, pl.ds(16 * h + 8, 8), :]
                return jnp.where(keep, a, pltpu.roll(b, 1, 0))

            def put(j, x):
                g_out[side, pl.ds(8 * j, 8), :] = x

            put_folded(put, get, tile_rows // 2)

    def take_g():
        for side in range(2):
            for q in range(tiles):
                for h in range(tile_rows // 2):
                    x = get_folded(lambda j: g_in[side, pl.ds(8 * j, 8), :], tile_rows // 2, q, h)
                    land_g[side, q, pl.ds(16 * h, 8), :] = x
                    land_g[side, q, pl.ds(16 * h + 8, 8), :] = pltpu.roll(x, 7, 0)

    def take_first(c):
        for copy in first_copies(c):
            copy.wait_recv()
        for side in range(2):
            for q in range(tiles):
                for h in range(tile_rows // 2):
                    x = get_folded(lambda j: first_in[side, c, pl.ds(8 * j, 8), :], tile_rows // 2, q, h)
                    field[1, c, ghost[side], q, at(2 * h), :] = x
                    field[1, c, ghost[side], q, at(2 * h + 1), :] = pltpu.roll(x, 7, 0)

    def send_theta(n, c):
        for side in range(2):
            red_here = facing(0, side)

            def get(q, i):
                x = field[0, c, rim[side], q, at(i), :]
                y = black(n)[c, rim[side], q, at(i), :]
                return jnp.where(red_here, x, y)

            def put(j, x):
                stage[n, side, c, pl.ds(8 * j, 8), :] = x

            put_folded(put, get, tile_rows)
        for copy in theta_copies(n, c):
            copy.start()

    zero_row = jnp.zeros((1, LANES), F32)
    zero = jnp.zeros((8, LANES), F32)

    def pack_s(k, _):
        for i in range(tile_rows):
            for q in range(tiles):
                a, b = raw_tile(raw_s, (2 * k,), i, q), raw_tile(raw_s, (2 * k + 1,), i, q)
                stiff[0, k + 1, q, at(i), :] = jnp.where(even, a, b)
                stiff[1, k + 1, q, at(i), :] = jnp.where(even, b, a)
        return 0

    def pack_d(k, _):
        for c in range(3):
            for i in range(tile_rows):
                for q in range(tiles):
                    a, b = raw_tile(raw_d, (c, 2 * k), i, q), raw_tile(raw_d, (c, 2 * k + 1), i, q)
                    field[0, c, k + 1, q, at(i), :] = jnp.where(even, a, b)
                    field[1, c, k + 1, q, at(i), :] = jnp.where(even, b, a)
        return 0

    def clear_rows(k, _):
        for c in range(3):
            for q in range(tiles):
                for row in beyond:
                    field[0, c, k + 1, q, one(row), :] = zero_row
                    last[c, k + 1, q, one(row), :] = zero_row
        return 0

    for c in rim_loads:
        c.wait()
    lax.fori_loop(0, 2, lambda j, _: pack_d(j * (pairs - 1), 0), 0)
    for c in range(3):
        pack_first(c)
    pl.semaphore_wait(barrier, len(greet))
    by_end(edge_corners, "start")
    for copy in edge_copies + [x for c in range(3) for x in first_copies(c)]:
        copy.start()
    load_s.wait()
    lax.fori_loop(0, pairs, pack_s, 0)
    by_end(stiff_rows, "start")
    load_d.wait()
    lax.fori_loop(1, pairs - 1, pack_d, 0)
    by_end(first_rows, "start")
    lax.fori_loop(0, pairs, clear_rows, 0)
    for end in range(2):
        @pl.when(jnp.logical_not(has[end]))
        def _():
            def clear(k, _):
                for q in range(tiles):
                    stiff[0, k + 1, q, one(beyond[end]), :] = zero_row
                    stiff[1, k + 1, q, one(beyond[end]), :] = zero_row
                    for c in range(3):
                        field[1, c, k + 1, q, one(beyond[end]), :] = zero_row
                return 0

            lax.fori_loop(0, pairs, clear, 0)
            for side in range(2):
                for q in range(tiles):
                    w_corner[side, end, q] = zero_row
                    w_face[side, end, q] = zero_row
                    for n in range(2):
                        for c in range(3):
                            corner[n, side, end, c, q] = zero_row

    for c in range(3):
        for g in ghost:
            for q in range(tiles):
                for i in range(tile_rows):
                    field[0, c, g, q, at(i), :] = zero
    load_w.wait()

    def beside(v, side):
        out = []
        for q in range(tiles):
            if side:
                x = pltpu.roll(v[q], LANES - 1, 1)
                if q < tiles - 1:
                    x = jnp.where(last_lane, pltpu.roll(v[q + 1], LANES - 1, 1), x)
            else:
                x = pltpu.roll(v[q], 1, 1)
                if q > 0:
                    x = jnp.where(first_lane, pltpu.roll(v[q - 1], 1, 1), x)
            out.append(x)
        return out

    def outer(colour, before, after):
        return jnp.where(even, before, after) if colour == 0 else jnp.where(even, after, before)

    def make_weights(colour, k):
        other = 1 - colour
        for i in range(tile_rows):
            mid = [stiff[other, k + 1, q, at(i), :] for q in range(tiles)]
            forth, back = beside(mid, 1), beside(mid, 0)
            for q in range(tiles):
                s = stiff[colour, k + 1, q, at(i), :]
                faces = [None] * 7
                faces[IN] = s + mid[q]
                faces[OUT] = s + outer(colour, stiff[other, k, q, at(i), :], stiff[other, k + 2, q, at(i), :])
                faces[RP] = s + stiff[other, k + 1, q, at(i, 1), :]
                faces[RM] = s + stiff[other, k + 1, q, at(i, -1), :]
                ap, am = forth[q], back[q]
                if q == tiles - 1:
                    ap = jnp.where(at_last_col, s, ap)
                if q == 0:
                    am = jnp.where(at_first_col, s, am)
                faces[AP], faces[AM] = s + ap, s + am
                total = faces[IN] + faces[OUT] + (faces[RP] + faces[RM]) + (faces[AP] + faces[AM])
                wa, wb = raw_tile(raw_w, (2 * k,), i, q), raw_tile(raw_w, (2 * k + 1,), i, q)
                fixed = (jnp.where(even, wa, wb) if colour == 0 else jnp.where(even, wb, wa)) != 0
                if q == tiles - 1 and last_lanes < LANES:
                    fixed = jnp.logical_or(fixed, jnp.logical_not(inside))
                scale = jnp.where(fixed, 0.0, 1.5 / total)
                put = pl.ds(8 * i, 8)
                if colour == 1:
                    scale_b[k, q, put, :] = scale
                weight[colour, SELF, k, q, put, :] = jnp.where(fixed, 1.0, -0.5)
                for f in (IN, OUT, RP, RM, AP, AM):
                    w = faces[f] * scale
                    if f == AP and q == tiles - 1:
                        w = jnp.where(at_last_col, 0.0, w)
                    if f == AM and q == 0:
                        w = jnp.where(at_first_col, 0.0, w)
                    weight[colour, f, k, q, put, :] = w

    def half(colour, k, opp, cur, dst, acc=None, comps=range(3)):
        for i in range(tile_rows):
            put = pl.ds(8 * i, 8)
            w = [[weight[colour, f, k, q, put, :] for q in range(tiles)] for f in range(7)]
            for c in comps:
                mid = [opp[c, k + 1, q, at(i), :] for q in range(tiles)]
                forth, back = beside(mid, 1), beside(mid, 0)
                for q in range(tiles):
                    far = outer(colour, opp[c, k, q, at(i), :], opp[c, k + 2, q, at(i), :])
                    old = cur[c, k + 1, q, at(i), :]
                    new = w[SELF][q] * old + w[IN][q] * mid[q] + w[OUT][q] * far
                    new = new + w[RP][q] * opp[c, k + 1, q, at(i, 1), :]
                    new = new + w[RM][q] * opp[c, k + 1, q, at(i, -1), :]
                    new = new + w[AP][q] * forth[q] + w[AM][q] * back[q]
                    if dst is not None:
                        dst[c, k + 1, q, at(i), :] = new
                    if acc is not None:
                        change = new - old
                        acc = acc + change * change
        return acc

    def inner(fn):
        lax.fori_loop(1, pairs - 1, lambda k, _: (fn(k), 0)[1], 0)

    def rims(fn):
        for k in (0, pairs - 1):
            fn(k)

    def face_weights():
        for side in range(2):
            k = rim[side]
            for q in range(tiles):
                for i in range(tile_rows):
                    put = pl.ds(8 * i, 8)
                    w_theta[side, q, put, :] = (stiff[1, ghost[side], q, at(i), :] + stiff[0, k, q, at(i), :]) * land_g[side, q, put, :]
        for end in range(2):
            @pl.when(has[end])
            def _():
                for q in range(tiles):
                    for side in range(2):
                        s = stiff[1, ghost[side], q, one(edge_row[end]), :]
                        g = land_g[side, q, one(edge_row[end] - OFF), :]
                        x = raw_row(edge_c, (side, end), q)
                        w_corner[side, end, q] = (s + x) * g
                        k = rim[side]
                        parity = (beyond[end] + lane) % 2 == 0
                        here = parity if side == 1 else jnp.logical_not(parity)
                        w_face[side, end, q] = jnp.where(here, (stiff[1, k, q, one(beyond[end]), :] + x) * rad_g[end, k - 1, q], 0.0)

    def rad_weights():
        for end in range(2):
            @pl.when(has[end])
            def _():
                def body(k, _):
                    for q in range(tiles):
                        w_rad[end, k, q] = (stiff[1, k + 1, q, one(beyond[end]), :] + stiff[0, k + 1, q, one(edge_row[end]), :]) * rad_g[end, k, q]
                    return 0

                for k in range(pairs):
                    body(k, 0)

    def cross_rad(n):
        dst = black(n)
        for end in range(2):
            @pl.when(has[end])
            def _():
                f = RP if end else RM

                def body(k, _):
                    for q in range(tiles):
                        w = weight[1, f, k, q, one(edge_row[end] - OFF), :]
                        wg = w_rad[end, k, q]
                        for c in range(3):
                            here = (c, k + 1, q, one(edge_row[end]), slice(None))
                            dst[here] = dst[here] + w * rad_in[n, 0, end, c, k, q]
                            dst[c, k + 1, q, one(beyond[end]), :] = rad_in[n, 1, end, c, k, q] + wg * field[(0, *here)]
                    return 0

                for k in range(pairs):
                    body(k, 0)

    def cross_theta(n, c):
        dst = black(n)
        for side in range(2):
            k, here = rim[side], facing(1, side)
            for q in range(tiles):
                for i in range(tile_rows):
                    put = pl.ds(8 * i, 8)
                    w = jnp.where(here, weight[1, OUT, k - 1, q, put, :], 0.0)
                    wg = w_theta[side, q, put, :]
                    x = get_folded(lambda j: land[n, side, c, pl.ds(8 * j, 8), :], tile_rows, q, i)
                    dst[c, k, q, at(i), :] = dst[c, k, q, at(i), :] + w * x
                    dst[c, ghost[side], q, at(i), :] = x + wg * field[0, c, k, q, at(i), :]
        for end in range(2):
            for side in range(2):
                for q in range(tiles):
                    x = corner[n, side, end, c, q]
                    a = (c, ghost[side], q, one(edge_row[end]), slice(None))
                    b = (c, rim[side], q, one(beyond[end]), slice(None))
                    dst[a] = dst[a] + w_corner[side, end, q] * x
                    dst[b] = dst[b] + w_face[side, end, q] * x

    red, black0 = field.at[0], field.at[1]

    by_end(stiff_rows, "take")
    inner(lambda k: (make_weights(0, k), make_weights(1, k)))
    by_end(first_rows, "take")
    inner(lambda k: half(0, k, black0, red, red))
    for copy in edge_copies:
        copy.wait_recv()
    for side in range(2):
        for i in range(tile_rows):
            for q in range(tiles):
                x = raw_tile(edge_s, (side,), i, q)
                stiff[0, ghost[side], q, at(i), :] = x
                stiff[1, ghost[side], q, at(i), :] = x
    rims(lambda k: (make_weights(0, k), make_weights(1, k)))
    pack_g()
    for copy in g_copies:
        copy.start()
    by_end(scale_rows, "start")
    by_end(first_rows, "drain")
    for c in range(3):
        take_first(c)
        rims(lambda k: half(0, k, black0, red, red, comps=(c,)))
        by_end(functools.partial(red_corners, 0, c), "start")
        rims(lambda k: half(1, k, red, black0, black0, comps=(c,)))
        send_theta(0, c)
    inner(lambda k: half(1, k, red, black0, black0))
    by_end(functools.partial(both_rows, 0), "start")

    by_end(scale_rows, "take")
    rad_weights()
    by_end(functools.partial(both_rows, 0), "take")
    by_end(functools.partial(both_rows, 0), "drain")
    cross_rad(0)
    for c in range(3):
        by_end(functools.partial(red_corners, 0, c), "drain")
    inner(lambda k: half(0, k, black0, red, red))
    for copy in g_copies:
        copy.wait_recv()
    take_g()
    by_end(edge_corners, "take")
    face_weights()
    for c in range(3):
        for copy in theta_copies(0, c):
            copy.wait_recv()
        by_end(functools.partial(red_corners, 0, c), "take")
        cross_theta(0, c)
        rims(lambda k: half(0, k, black0, red, red, comps=(c,)))
        by_end(functools.partial(red_corners, 1, c), "start")
        rims(lambda k: half(1, k, red, black0, last, comps=(c,)))
        send_theta(1, c)
    inner(lambda k: half(1, k, red, black0, last))
    by_end(functools.partial(both_rows, 1), "start")

    def squares(k, acc, comps=range(3)):
        for i in range(tile_rows):
            for q in range(tiles):
                for c in comps:
                    change = last[c, k + 1, q, at(i), :] - field[1, c, k + 1, q, at(i), :]
                    acc = acc + change * change
        return acc

    by_end(functools.partial(both_rows, 1), "take")
    by_end(functools.partial(both_rows, 1), "drain")
    cross_rad(1)
    red_sum = lax.fori_loop(1, pairs - 1, lambda k, a: half(0, k, last, red, None, a), zero)
    black_sum = lax.fori_loop(1, pairs - 1, squares, zero)
    for c in range(3):
        for copy in theta_copies(1, c):
            copy.wait_recv()
        by_end(functools.partial(red_corners, 1, c), "take")
        cross_theta(1, c)
        for k in (0, pairs - 1):
            red_sum = half(0, k, last, red, None, red_sum, comps=(c,))
            black_sum = squares(k, black_sum, comps=(c,))

    part[0] = jnp.sum(black_sum * (1.0 / 9.0) + red_sum * (1.0 / 2.25), axis=0, keepdims=True)
    for level, peers in enumerate(groups):
        for j, p in enumerate(peers):
            pltpu.make_async_remote_copy(
                part.at[level], gather.at[level, pl.ds(j, 1)], ar_send.at[level], ar_recv.at[level], device_id=p, device_id_type=MESH
            ).start()
        if level == 0:
            def unpack(j, _):
                c, k = j // pairs, j % pairs
                for i in range(tile_rows):
                    for q in range(tiles):
                        a, b = field[0, c, k + 1, q, at(i), :], last[c, k + 1, q, at(i), :]
                        x, y = jnp.where(even, a, b), jnp.where(even, b, a)
                        n = LANES if q < tiles - 1 else last_lanes
                        raw_d[c, 2 * k, pl.ds(8 * i, 8), pl.ds(q * LANES, n)] = x[:, :n]
                        raw_d[c, 2 * k + 1, pl.ds(8 * i, 8), pl.ds(q * LANES, n)] = y[:, :n]
                return 0

            lax.fori_loop(0, 3 * pairs, unpack, 0)
            pltpu.make_async_copy(raw_d, out_hbm, out_sem.at[0]).start()
        everything = gather.at[level, pl.ds(0, len(peers))]
        pltpu.make_async_copy(everything, everything, ar_recv.at[level]).wait()
        part[level + 1] = part[level] + jnp.sum(gather[level, : len(peers)], axis=0, keepdims=True)
    norm_ref[...] = jnp.sqrt(jnp.sum(part[len(groups)], keepdims=True) / count)

    for level, peers in enumerate(groups):
        everything = gather.at[level, pl.ds(0, len(peers))]
        pltpu.make_async_copy(everything, everything, ar_send.at[level]).wait()
    for copy in edge_copies + g_copies + [x for c in range(3) for x in first_copies(c) + theta_copies(0, c) + theta_copies(1, c)]:
        copy.wait_send()
    for copies in (stiff_rows, edge_corners, scale_rows, *(functools.partial(red_corners, 1, c) for c in range(3))):
        by_end(copies, "drain")
    pltpu.make_async_copy(raw_d, out_hbm, out_sem.at[0]).wait()


def make_levels(n_theta, n_rad):
    plane = 8 if n_theta % 8 == 0 else n_theta
    stacks = n_theta // plane

    def within(t, r):
        z, x = t // plane, lax.rem(t, plane)
        return [
            (z * plane + lax.rem(x + i, plane), lax.rem(r + j, n_rad))
            for j in range(n_rad) for i in range(plane) if i or j
        ]

    def across(t, r):
        return [(lax.rem(t + i * plane, n_theta), r) for i in range(1, stacks)]

    return (within, across), (n_rad * plane - 1, stacks - 1)


def solution(mesh):
    n_theta, n_rad = mesh.shape["theta"], mesh.shape["rad"]
    levels, sizes = make_levels(n_theta, n_rad)

    def shards(displacement, stiffness, wall):
        planes, rows, cols = stiffness.shape
        pairs, tiles = planes // 2, -(-cols // LANES)
        folded = (tiles - 1) * rows + rows // 2
        count = 3.0 * planes * rows * cols * n_theta * n_rad
        cfg = (n_theta, n_rad, pairs, rows, cols, tiles, levels, count)
        dma = pltpu.SemaphoreType.DMA
        moved, norm = pl.pallas_call(
            functools.partial(kernel, cfg),
            out_shape=(pltpu.VMEM(displacement.shape, F32), jax.ShapeDtypeStruct((1, 1), F32)),
            in_specs=[pl.BlockSpec(memory_space=pl.ANY)] * 3,
            out_specs=(pl.BlockSpec(memory_space=pl.ANY), pl.BlockSpec(memory_space=pltpu.VMEM)),
            scratch_shapes=[
                pltpu.VMEM((3, planes, rows, cols), F32),
                pltpu.VMEM((planes, rows, cols), F32),
                pltpu.VMEM((planes, rows, cols), jnp.int32),
                pltpu.VMEM((2, 3, pairs + 2, tiles, rows + 16, LANES), F32),
                pltpu.VMEM((3, pairs + 2, tiles, rows + 16, LANES), F32),
                pltpu.VMEM((2, pairs + 2, tiles, rows + 16, LANES), F32),
                pltpu.VMEM((2, 7, pairs, tiles, rows, LANES), F32),
                pltpu.VMEM((pairs, tiles, rows, LANES), F32),
                pltpu.VMEM((2, 3, folded // 2, LANES), F32),
                pltpu.VMEM((2, 3, folded // 2, LANES), F32),
                pltpu.VMEM((2, 2, 3, folded, LANES), F32),
                pltpu.VMEM((2, 2, 3, folded, LANES), F32),
                pltpu.VMEM((2, folded // 2, LANES), F32),
                pltpu.VMEM((2, folded // 2, LANES), F32),
                pltpu.VMEM((2, tiles, rows, LANES), F32),
                pltpu.VMEM((2, 2, 2, 3, pairs, tiles, 1, LANES), F32),
                pltpu.VMEM((2, pairs, tiles, 1, LANES), F32),
                pltpu.VMEM((2, 2, 2, 3, tiles, 1, LANES), F32),
                pltpu.VMEM((2, rows, cols), F32),
                pltpu.VMEM((2, 2, 1, cols), F32),
                pltpu.VMEM((2, tiles, rows, LANES), F32),
                pltpu.VMEM((2, pairs, tiles, 1, LANES), F32),
                pltpu.VMEM((2, 2, tiles, 1, LANES), F32),
                pltpu.VMEM((2, 2, tiles, 1, LANES), F32),
                pltpu.VMEM((3, 1, LANES), F32),
                pltpu.VMEM((2, -(-max(sizes) // 8) * 8, LANES), F32),
                dma((5,)), dma((1,)), dma((3, 2)), dma((3, 2)), dma((2, 3, 2)), dma((2, 3, 2)), dma((2,)), dma((2,)),
                dma((2,)), dma((2,)), dma((2, 2)), dma((2, 2)), dma((2, 2)), dma((2, 2)), dma((2,)), dma((2,)),
                dma((2, 2, 2)), dma((2, 2, 2)), dma((2,)), dma((2,)), dma((2, 3, 2, 2)), dma((2, 3, 2, 2)), dma((2,)), dma((2,)),
            ],
            compiler_params=pltpu.CompilerParams(collective_id=0, has_side_effects=True, vmem_limit_bytes=56 * 2**20),
            cost_estimate=pl.CostEstimate(flops=10**8, bytes_accessed=4 * 10**6, transcendentals=0),
        )(displacement, stiffness, wall)
        return moved, norm.reshape(())

    placed = (P(None, "theta", "rad", None), P("theta", "rad", None), P("theta", "rad", None))
    return jax.shard_map(
        shards, mesh=mesh, in_specs=placed, out_specs=(P(None, "theta", "rad", None), P()), check_vma=False,
    )
```
